32 devices in a mesh: outer: 8 (over y, x, core), inner: 4 (over z).
Axes of the slice: x: 2, y: 2, z: 4, core: 2. Of those that a mesh axis runs over, the one named last changes fastest.
Arguments:
- queries: bfloat16 [8192, 1536], P(('outer', 'inner')), may hold values from -6 to 6
- key_rows: bfloat16 [8192, 1536], P(('outer', 'inner')), may hold values from -6 to 6
- values: bfloat16 [8192, 1536], P(('outer', 'inner')), may hold values from -6 to 6
- out_grads: bfloat16 [8192, 1536], P(('outer', 'inner')), may hold values from -96 to 96
- offsets: int32 [8], replicated, may hold values from 0 to 127, as said below
Outputs:
- grad_queries: bfloat16 [8192, 1536], P(('outer', 'inner'))
- grad_keys: bfloat16 [8192, 1536], P(('outer', 'inner'))
- grad_values: bfloat16 [8192, 1536], P(('outer', 'inner'))
The draws below stay inside these ranges and needn't reach their ends.
Inputs may be any that keep to these rules, and one draw needn't show every extreme that they name: offsets[j] is below 4 for j < 5 and below 128 for the others.
All inputs are finite; a program needn't handle non-finite values.
Results may differ from the reference program's by a relative error of at most 0.0057.
The reference program's roundings to bfloat16 on the way count: a program that leaves them out, or rounds other values in their place, can miss the bound.
Values may be sent and summed in bfloat16 or wider, within the bound.
A program may use at most 64 MiB of HBM per device.

```python
import math
import jax
import jax.numpy as jnp
from jax import lax

HEAD_DIM = 128
H_NEAR = 4
H_MID = 5
H_WIDE = 3
HEADS = 12
R_MID = 4
R_WIDE = 128
TOK_DEV = 256
SEG_MID = 1024
TOKENS = 8192


def draw_queries(key, part):
    key = jax.random.fold_in(key, 7)
    drawn = jnp.clip(jax.random.normal(key, (TOKENS, HEADS * HEAD_DIM)), -6.0, 6.0)
    return drawn.astype(jnp.bfloat16)


def draw_key_rows(key, part):
    key = jax.random.fold_in(key, 8)
    drawn = jnp.clip(jax.random.normal(key, (TOKENS, HEADS * HEAD_DIM)), -6.0, 6.0)
    return drawn.astype(jnp.bfloat16)


def draw_offsets(key, part):
    key = jax.random.fold_in(key, 9)
    heads_all = H_MID + H_WIDE
    limits = jnp.where(jnp.arange(heads_all) < H_MID, R_MID, R_WIDE).astype(jnp.int32)
    drawn = jax.random.randint(key, (heads_all,), 0, limits).astype(jnp.int32)
    low_head = jax.random.randint(jax.random.fold_in(key, 11), (), 0, H_MID).astype(jnp.int32)
    high_head = jax.random.randint(jax.random.fold_in(key, 12), (), H_MID, heads_all).astype(jnp.int32)
    position = jnp.arange(heads_all, dtype=jnp.int32)
    drawn = jnp.where(position == low_head, jnp.zeros((), jnp.int32), drawn)
    drawn = jnp.where(position == high_head, jnp.full((), R_WIDE - 1, jnp.int32), drawn)
    return drawn.astype(jnp.int32)


def block_levels(rng, dims, pieces, low, top_value):
    loudness = 1.0
    for axis_at, shards_of in pieces:
        heights = jax.random.uniform(jax.random.fold_in(jax.random.fold_in(rng, 6), axis_at), (shards_of,), jnp.float32, low / len(pieces), top_value / len(pieces))
        loudness = loudness * jnp.repeat(jnp.exp(heights), dims[axis_at] // shards_of).reshape((-1,) + (1,) * (len(dims) - 1 - axis_at))
    return loudness


def gaussian(stream_key, shape, width, limit, pieces=(), kind=jnp.bfloat16):
    result = width * jax.random.normal(stream_key, shape, jnp.float32)
    if pieces:
        result = result * block_levels(stream_key, shape, pieces, -0.22, 0.18)
    return jnp.clip(result, -limit, limit).astype(kind)


def setup_inputs(seed: int = 0) -> dict:
    arg_keys = jax.random.split(jax.random.key(seed), 6)
    return {
        "queries": draw_queries(jax.random.fold_in(arg_keys[5], 71), 0),
        "key_rows": draw_key_rows(jax.random.fold_in(arg_keys[5], 71), 0),
        "values": gaussian(arg_keys[2], (TOKENS, HEADS * HEAD_DIM), 1.0, 6.0, ((0, 32),)),
        "out_grads": gaussian(arg_keys[3], (TOKENS, HEADS * HEAD_DIM), 16.0, 96.0, ((0, 32),)),
        "offsets": draw_offsets(jax.random.fold_in(arg_keys[5], 71), 0),
    }


def rounded(tensor):
    return lax.optimization_barrier(tensor.astype(jnp.bfloat16)).astype(jnp.float32)

def select_rows(block, head_offsets, stride):
    row_number, columns = block.shape
    head_count = head_offsets.shape[0]
    shaped = block.reshape(row_number // stride, stride, head_count, columns // head_count)
    chosen = jnp.arange(stride, dtype=jnp.int32)[:, None] == head_offsets[None, :].astype(jnp.int32)
    masked = jnp.where(chosen[None, :, :, None], shaped, jnp.zeros((), block.dtype))
    return lax.optimization_barrier(jnp.sum(masked, axis=1)).astype(block.dtype)

def spread_rows(picked, head_offsets, stride):
    picked_rows, head_count, head_depth = picked.shape
    chosen = jnp.arange(stride, dtype=jnp.int32)[:, None] == head_offsets[None, :].astype(jnp.int32)
    placed = jnp.where(chosen[None, :, :, None], picked[:, None], jnp.zeros((), picked.dtype))
    return placed.reshape(picked_rows * stride, head_count * head_depth)

def backward_full(blocks):
    query_row_block, key_tile_block, value_tile_block, gradient_rows = [part.astype(jnp.float32) for part in blocks]
    score_scale = 1.0 / math.sqrt(query_row_block.shape[-1])
    logit_scores = jnp.einsum('agk,igk->gai', query_row_block, key_tile_block) * score_scale
    row_max = lax.optimization_barrier(jnp.max(logit_scores, axis=2, keepdims=True))
    exponent = jnp.exp(logit_scores - row_max)
    weights = exponent / lax.optimization_barrier(jnp.sum(exponent, axis=2, keepdims=True))
    product_gradients = jnp.einsum('agk,igk->gai', gradient_rows, value_tile_block)
    row_dots = lax.optimization_barrier(jnp.sum(weights * product_gradients, axis=2, keepdims=True))
    weights_bfloat = rounded(weights)
    score_gradients = rounded(weights * (product_gradients - row_dots) * score_scale)
    query_gradient = jnp.einsum('ywr,ryu->wyu', score_gradients, key_tile_block)
    key_gradient = jnp.einsum('wfl,fwp->lwp', score_gradients, query_row_block)
    value_gradient = jnp.einsum('wfl,fwp->lwp', weights_bfloat, gradient_rows)
    return (query_gradient, key_gradient, value_gradient)

def reference(queries, key_rows, values, out_grads, offsets):
    near_end = H_NEAR * HEAD_DIM
    mid_end = near_end + H_MID * HEAD_DIM
    arrays = (queries, key_rows, values, out_grads)
    near_parts = tuple((block[:, :near_end].reshape(TOKENS // TOK_DEV, TOK_DEV, H_NEAR, HEAD_DIM) for block in arrays))
    near_result = lax.map(backward_full, near_parts)
    near_result = [part.reshape(TOKENS, near_end) for part in near_result]
    mid_offsets = offsets[:H_MID]
    wide_offsets = offsets[H_MID:]
    segments = TOKENS // SEG_MID
    mid_parts = tuple((select_rows(block[:, near_end:mid_end], mid_offsets, R_MID).reshape(segments, SEG_MID // R_MID, H_MID, HEAD_DIM) for block in arrays))
    mid_result = lax.map(backward_full, mid_parts)
    mid_result = [spread_rows(part.reshape(TOKENS // R_MID, H_MID, HEAD_DIM), mid_offsets, R_MID) for part in mid_result]
    wide_parts = tuple((select_rows(block[:, mid_end:], wide_offsets, R_WIDE) for block in arrays))
    wide_result = backward_full(wide_parts)
    wide_result = [spread_rows(part, wide_offsets, R_WIDE) for part in wide_result]
    joined = [jnp.concatenate([near_result[index], mid_result[index], wide_result[index]], axis=1).astype(jnp.bfloat16) for index in range(3)]
    return (joined[0], joined[1], joined[2])
```

```python
import functools
import math

import jax
import jax.numpy as jnp
from jax import lax
from jax.experimental import pallas as pl
from jax.experimental.pallas import tpu as pltpu
from jax.sharding import PartitionSpec as P

HEAD_DIM = 128
H_NEAR = 4
H_MID = 5
H_WIDE = 3
HEADS = H_NEAR + H_MID + H_WIDE
R_MID = 4
R_WIDE = 128
NEAR_END = H_NEAR * HEAD_DIM
MID_END = NEAR_END + H_MID * HEAD_DIM
WIDE_ROWS = 8
MESH = pl.DeviceIdType.MESH
F32 = jnp.float32
BF16 = jnp.bfloat16


def dot(left, right, contract):
    return lax.dot_general(left, right, ((contract[:1], contract[1:]), ((), ())), preferred_element_type=F32)


def attention_parts(q, k, v, g, mask=None):
    scale = 1.0 / math.sqrt(HEAD_DIM)
    scores = dot(q, k, (1, 1)) * scale
    if mask is not None:
        scores = jnp.where(mask, scores, -1e30)
    exponent = jnp.exp(scores - jnp.max(scores, axis=1, keepdims=True))
    weights = exponent * (1.0 / jnp.sum(exponent, axis=1, keepdims=True))
    dots = dot(g, v, (1, 1))
    row_dots = jnp.sum(weights * dots, axis=1, keepdims=True)
    score_grads = (weights * (dots - row_dots) * scale).astype(BF16)
    return weights.astype(BF16), score_grads


def kernel(
    n_outer, n_inner, offsets, queries, key_rows, values, out_grads, grad_q, grad_k, grad_v,
    x, y, picked, arrived, result, returned, wide, wide_result,
    in_sem, out_sem, mid_send, mid_recv, back_send, back_recv,
    line_send, line_recv, plane_send, plane_recv,
):
    tokens = x.shape[1]
    rows = tokens // R_MID
    wide_tokens = tokens // R_WIDE
    slots = arrived.shape[0]
    me_o, me_i = lax.axis_index("outer"), lax.axis_index("inner")
    inputs = (queries, key_rows, values, out_grads)
    outputs = (grad_q, grad_k, grad_v)

    def inner_peer(step):
        return lax.rem(me_i + step, n_inner)

    def outer_peer(step):
        return lax.rem(me_o + step, n_outer)

    spans = (pl.ds(NEAR_END, HEADS * HEAD_DIM - NEAR_END), pl.ds(0, NEAR_END))
    loads = [
        [
            pltpu.make_async_copy(inputs[a].at[:, span], x.at[a, :, span], in_sem.at[s, a])
            for a in range(4)
        ]
        for s, span in enumerate(spans)
    ]
    for group in loads:
        for load in group:
            load.start()

    barrier = pltpu.get_barrier_semaphore()
    for step in range(1, n_inner):
        pl.semaphore_signal(barrier, inc=1, device_id=(me_o, inner_peer(step)), device_id_type=MESH)
    for step in range(1, n_outer):
        pl.semaphore_signal(barrier, inc=1, device_id=(outer_peer(step), me_i), device_id_type=MESH)

    for load in loads[0]:
        load.wait()

    position = lax.broadcasted_iota(jnp.int32, (16, tokens), 1)
    row = lax.broadcasted_iota(jnp.int32, (16, tokens), 0)
    chosen = jnp.zeros((16, tokens), jnp.bool_)
    for head in range(H_WIDE):
        for token in range(wide_tokens):
            at = token * R_WIDE + offsets[H_MID + head]
            chosen = chosen | ((row == head * wide_tokens + token) & (position == at))
    chosen = chosen.astype(F32).astype(BF16)
    head_of = lax.broadcasted_iota(jnp.int32, (WIDE_ROWS, HEAD_DIM), 0) // wide_tokens
    blocks = []
    for a in range(4):
        both = dot(chosen, x[a, :, MID_END:], (1, 0))[:WIDE_ROWS]
        block = jnp.zeros((WIDE_ROWS, HEAD_DIM), F32)
        for head in range(H_WIDE):
            part = both[:, head * HEAD_DIM:(head + 1) * HEAD_DIM]
            block = jnp.where(head_of == head, part, block)
        blocks.append(block)
    wide[me_o, me_i] = jnp.concatenate(blocks, axis=0).astype(BF16)

    pl.semaphore_wait(barrier, n_inner - 1 + n_outer - 1)

    def line_copy(step, source):
        return pltpu.make_async_remote_copy(
            src_ref=wide.at[me_o, me_i], dst_ref=wide.at[me_o, source],
            send_sem=line_send.at[step], recv_sem=line_recv.at[source],
            device_id=(me_o, inner_peer(step)), device_id_type=MESH,
        )

    for step in range(1, n_inner):
        line_copy(step, me_i).start()

    def owner(head):
        if head < n_inner:
            return jnp.int32(head)
        return lax.rem(head % n_inner + n_inner // 2 + n_inner - lax.rem(me_o, 2), n_inner)

    def mid_copy(head, slot, source, target):
        return pltpu.make_async_remote_copy(
            src_ref=picked.at[head], dst_ref=arrived.at[slot, source],
            send_sem=mid_send.at[head], recv_sem=mid_recv.at[slot, source],
            device_id=(me_o, target), device_id_type=MESH,
        )

    pick_row = lax.broadcasted_iota(jnp.int32, (rows, tokens), 0)
    pick_position = lax.broadcasted_iota(jnp.int32, (rows, tokens), 1)
    for head in range(H_MID):
        pick = (pick_position == pick_row * R_MID + offsets[head]).astype(F32).astype(BF16)
        columns = slice(NEAR_END + head * HEAD_DIM, NEAR_END + (head + 1) * HEAD_DIM)
        for a in range(4):
            picked[head, a] = dot(pick, x[a, :, columns], (1, 0)).astype(BF16)
        target = owner(head)

        @pl.when(me_i != target)
        def _():
            mid_copy(head, head // n_inner, me_i, target).start()

        @pl.when(me_i == target)
        def _():
            arrived[head // n_inner, me_i] = picked[head]

    for load in loads[1]:
        load.wait()

    def near_head(head, carry):
        columns = pl.ds(pl.multiple_of(head * HEAD_DIM, HEAD_DIM), HEAD_DIM)
        q, k, v, g = [x[a, :, columns] for a in range(4)]
        weights, score_grads = attention_parts(q, k, v, g)
        y[0, :, columns] = dot(score_grads, k, (1, 0)).astype(BF16)
        y[1, :, columns] = dot(score_grads, q, (0, 0)).astype(BF16)
        y[2, :, columns] = dot(weights, g, (0, 0)).astype(BF16)
        return carry

    lax.fori_loop(0, H_NEAR // 2, near_head, 0)

    for step in range(1, n_inner):
        line_copy(step, inner_peer(step)).wait_recv()

    def plane_copy(step, source):
        return pltpu.make_async_remote_copy(
            src_ref=wide.at[me_o], dst_ref=wide.at[source],
            send_sem=plane_send.at[step], recv_sem=plane_recv.at[source],
            device_id=(outer_peer(step), me_i), device_id_type=MESH,
        )

    for step in range(1, n_outer):
        plane_copy(step, me_o).start()

    lax.fori_loop(H_NEAR // 2, H_NEAR, near_head, 0)

    def store(group, span):
        return [
            pltpu.make_async_copy(y.at[which, :, span], outputs[which].at[:, span], out_sem.at[group, which])
            for which in range(3)
        ]

    stores = store(0, spans[1])
    for copy in stores:
        copy.start()

    for step in range(1, n_outer):
        plane_copy(step, outer_peer(step)).wait_recv()
    devices = n_outer * n_inner
    total = devices * WIDE_ROWS
    tile = min(total, 256)

    def gathered(a, start, count):
        block = wide[...].reshape(devices, 4 * WIDE_ROWS, HEAD_DIM).astype(F32)
        return block[start:start + count, a * WIDE_ROWS:(a + 1) * WIDE_ROWS].reshape(
            count * WIDE_ROWS, HEAD_DIM).astype(BF16)

    wide_k, wide_v = gathered(1, 0, devices), gathered(2, 0, devices)
    wide_result[...] = jnp.zeros_like(wide_result)
    for first in range(0, total, tile):
        q = gathered(0, first // WIDE_ROWS, tile // WIDE_ROWS)
        g = gathered(3, first // WIDE_ROWS, tile // WIDE_ROWS)
        query_head = lax.rem(lax.broadcasted_iota(jnp.int32, (tile, total), 0), WIDE_ROWS) // wide_tokens
        key_head = lax.rem(lax.broadcasted_iota(jnp.int32, (tile, total), 1), WIDE_ROWS) // wide_tokens
        weights, score_grads = attention_parts(q, wide_k, wide_v, g, query_head == key_head)
        wide_result[0, first:first + tile] = dot(score_grads, wide_k, (1, 0))
        wide_result[1] += dot(score_grads, q, (0, 0))
        wide_result[2] += dot(weights, g, (0, 0))
    mine = pl.ds(pl.multiple_of((me_o * n_inner + me_i) * WIDE_ROWS, WIDE_ROWS), WIDE_ROWS)
    place = lax.broadcasted_iota(jnp.int32, (tokens, HEAD_DIM), 0)
    for which in range(3):
        block = wide_result[which, mine, :]
        for head in range(H_WIDE):
            spread = jnp.zeros((tokens, HEAD_DIM), F32)
            for token in range(wide_tokens):
                at = head * wide_tokens + token
                spread = jnp.where(
                    place == token * R_WIDE + offsets[H_MID + head], block[at:at + 1], spread
                )
            first = MID_END + head * HEAD_DIM
            y[which, :, first:first + HEAD_DIM] = spread.astype(BF16)

    def back_copy(slot, head, source):
        return pltpu.make_async_remote_copy(
            src_ref=result.at[slot, source], dst_ref=returned.at[head],
            send_sem=back_send.at[slot, source], recv_sem=back_recv.at[head],
            device_id=(me_o, source), device_id_type=MESH,
        )

    def owned(slot):
        if slot == 0:
            return me_i
        shift = lax.rem(me_i + 2 * n_inner - n_inner // 2 + lax.rem(me_o, 2), n_inner)
        return slot * n_inner + shift

    segment = n_inner * rows
    for slot in range(slots):
        head = owned(slot)

        @pl.when(head < H_MID)
        def _():
            for step in range(1, n_inner):
                source = inner_peer(step)
                mid_copy(0, slot, source, source).wait_recv()
            q, k, v, g = [arrived[slot, :, a].reshape(segment, HEAD_DIM) for a in range(4)]
            weights, score_grads = attention_parts(q, k, v, g)
            grads = (
                dot(score_grads, k, (1, 0)), dot(score_grads, q, (0, 0)), dot(weights, g, (0, 0))
            )
            for which in range(3):
                result[slot, :, which] = grads[which].astype(BF16).reshape(n_inner, rows, HEAD_DIM)
            for step in range(1, n_inner):
                back_copy(slot, head, inner_peer(step)).start()
            returned[head] = result[slot, me_i]

    spread_row = lax.broadcasted_iota(jnp.int32, (tokens, rows), 1)
    spread_position = lax.broadcasted_iota(jnp.int32, (tokens, rows), 0)
    for head in range(H_MID):
        target = owner(head)

        @pl.when(me_i != target)
        def _():
            back_copy(0, head, target).wait_recv()

        place = (spread_position == spread_row * R_MID + offsets[head]).astype(F32).astype(BF16)
        columns = slice(NEAR_END + head * HEAD_DIM, NEAR_END + (head + 1) * HEAD_DIM)
        for which in range(3):
            y[which, :, columns] = dot(place, returned[head, which], (1, 0)).astype(BF16)

    last = store(1, spans[0])
    for copy in last:
        copy.start()

    for step in range(1, n_inner):
        line_copy(step, me_i).wait_send()
    for step in range(1, n_outer):
        plane_copy(step, me_o).wait_send()
    for head in range(H_MID):
        target = owner(head)

        @pl.when(me_i != target)
        def _():
            mid_copy(head, 0, me_i, target).wait_send()

    for slot in range(slots):
        head = owned(slot)

        @pl.when(head < H_MID)
        def _():
            for step in range(1, n_inner):
                back_copy(slot, head, inner_peer(step)).wait_send()

    for copy in stores + last:
        copy.wait()


def body(n_outer, n_inner, queries, key_rows, values, out_grads, offsets):
    tokens, columns = queries.shape
    rows = tokens // R_MID
    slots = -(-H_MID // n_inner)
    anywhere = pl.BlockSpec(memory_space=pl.ANY)
    dma = pltpu.SemaphoreType.DMA
    return tuple(pl.pallas_call(
        functools.partial(kernel, n_outer, n_inner),
        out_shape=[jax.ShapeDtypeStruct((tokens, columns), BF16)] * 3,
        in_specs=[pl.BlockSpec(memory_space=pltpu.SMEM)] + [anywhere] * 4,
        out_specs=[anywhere] * 3,
        scratch_shapes=[
            pltpu.VMEM((4, tokens, columns), BF16),
            pltpu.VMEM((3, tokens, columns), BF16),
            pltpu.VMEM((H_MID, 4, rows, HEAD_DIM), BF16),
            pltpu.VMEM((slots, n_inner, 4, rows, HEAD_DIM), BF16),
            pltpu.VMEM((slots, n_inner, 3, rows, HEAD_DIM), BF16),
            pltpu.VMEM((H_MID, 3, rows, HEAD_DIM), BF16),
            pltpu.VMEM((n_outer, n_inner, 4 * WIDE_ROWS, HEAD_DIM), BF16),
            pltpu.VMEM((3, n_outer * n_inner * WIDE_ROWS, HEAD_DIM), F32),
            dma((2, 4)),
            dma((2, 3)),
            dma((H_MID,)),
            dma((slots, n_inner)),
            dma((slots, n_inner)),
            dma((H_MID,)),
            dma((n_inner,)),
            dma((n_inner,)),
            dma((n_outer,)),
            dma((n_outer,)),
        ],
        compiler_params=pltpu.CompilerParams(
            collective_id=0, has_side_effects=True, vmem_limit_bytes=48 * 1024 * 1024
        ),
    )(offsets, queries, key_rows, values, out_grads))


def solution(mesh):
    split = P(("outer", "inner"), None)
    return jax.shard_map(
        functools.partial(body, mesh.shape["outer"], mesh.shape["inner"]),
        mesh=mesh,
        in_specs=(split, split, split, split, P()),
        out_specs=(split,) * 3,
        check_vma=False,
    )
```

```python
import functools
import math

import jax
import jax.numpy as jnp
from jax import lax
from jax.experimental import pallas as pl
from jax.experimental.pallas import tpu as pltpu
from jax.sharding import PartitionSpec as P

HEAD_DIM = 128
H_NEAR = 4
H_MID = 5
H_WIDE = 3
HEADS = H_NEAR + H_MID + H_WIDE
R_MID = 4
R_WIDE = 128
NEAR_END = H_NEAR * HEAD_DIM
MID_END = NEAR_END + H_MID * HEAD_DIM
WIDE_ROWS = 8
MESH = pl.DeviceIdType.MESH
F32 = jnp.float32
BF16 = jnp.bfloat16


def dot(left, right, contract):
    return lax.dot_general(left, right, ((contract[:1], contract[1:]), ((), ())), preferred_element_type=F32)


def attention_parts(q, k, v, g, mask=None):
    scale = 1.0 / math.sqrt(HEAD_DIM)
    scores = dot(q, k, (1, 1)) * scale
    if mask is not None:
        scores = jnp.where(mask, scores, -1e30)
    exponent = jnp.exp(scores - jnp.max(scores, axis=1, keepdims=True))
    weights = exponent * (1.0 / jnp.sum(exponent, axis=1, keepdims=True))
    dots = dot(g, v, (1, 1))
    row_dots = jnp.sum(weights * dots, axis=1, keepdims=True)
    score_grads = (weights * (dots - row_dots) * scale).astype(BF16)
    return weights.astype(BF16), score_grads


def kernel(
    n_outer, n_inner, offsets_in, queries, key_rows, values, out_grads, grad_q, grad_k, grad_v,
    offsets, x, y, picked, arrived, result, returned, wide, wide_result,
    offsets_sem, in_sem, out_sem, mid_send, mid_recv, back_send, back_recv,
    line_send, line_recv, plane_send, plane_recv,
):
    tokens = x.shape[1]
    rows = tokens // R_MID
    wide_tokens = tokens // R_WIDE
    slots = arrived.shape[0]
    me_o, me_i = lax.axis_index("outer"), lax.axis_index("inner")
    inputs = (queries, key_rows, values, out_grads)
    outputs = (grad_q, grad_k, grad_v)

    def inner_peer(step):
        return lax.rem(me_i + step, n_inner)

    def outer_peer(step):
        return lax.rem(me_o + step, n_outer)

    first_head = jnp.where(me_i < n_inner // 2, n_inner // 2, n_inner)

    def head_at(step):
        return lax.rem(first_head + step, H_MID)

    def head_columns(head):
        return pl.ds(pl.multiple_of(NEAR_END + head * HEAD_DIM, HEAD_DIM), HEAD_DIM)

    def load(group, span):
        return [
            pltpu.make_async_copy(inputs[a].at[:, span], x.at[a, :, span], in_sem.at[group, a])
            for a in range(4)
        ]

    near_span, wide_span = pl.ds(0, NEAR_END), pl.ds(MID_END, H_WIDE * HEAD_DIM)
    offsets_load = pltpu.make_async_copy(offsets_in, offsets, offsets_sem)
    offsets_load.start()
    loads = [load(step, head_columns(head_at(step))) for step in range(H_MID)]
    loads += [load(H_MID, wide_span), load(H_MID + 1, near_span)]
    for group in loads:
        for copy in group:
            copy.start()

    barrier = pltpu.get_barrier_semaphore()
    for step in range(1, n_inner):
        pl.semaphore_signal(barrier, inc=1, device_id=(me_o, inner_peer(step)), device_id_type=MESH)
    for step in range(1, n_outer):
        pl.semaphore_signal(barrier, inc=1, device_id=(outer_peer(step), me_i), device_id_type=MESH)

    def owner(head):
        turned = head + n_inner // 2 + n_inner - lax.rem(me_o, 2)
        return jnp.where(head < n_inner, head, lax.rem(turned, n_inner))

    def mid_copy(head, slot, source, target):
        return pltpu.make_async_remote_copy(
            src_ref=picked.at[head], dst_ref=arrived.at[slot, source],
            send_sem=mid_send.at[head], recv_sem=mid_recv.at[slot, source],
            device_id=(me_o, target), device_id_type=MESH,
        )

    pick_row = lax.broadcasted_iota(jnp.int32, (rows, tokens), 0)
    pick_position = lax.broadcasted_iota(jnp.int32, (rows, tokens), 1)

    def pick_head(step):
        for copy in loads[step]:
            copy.wait()
        head = head_at(step)
        pick = (pick_position == pick_row * R_MID + offsets[head]).astype(F32).astype(BF16)
        for a in range(4):
            picked[head, a] = dot(pick, x[a, :, head_columns(head)], (1, 0)).astype(BF16)

    def send_head(step):
        head = head_at(step)
        target, slot = owner(head), head // n_inner

        @pl.when(me_i != target)
        def _():
            mid_copy(head, slot, me_i, target).start()

        @pl.when(me_i == target)
        def _():
            arrived[slot, me_i] = picked[head]

    offsets_load.wait()
    pick_head(0)
    pl.semaphore_wait(barrier, n_inner - 1 + n_outer - 1)
    send_head(0)
    pick_head(1)
    send_head(1)

    for copy in loads[H_MID]:
        copy.wait()
    position = lax.broadcasted_iota(jnp.int32, (16, tokens), 1)
    row = lax.broadcasted_iota(jnp.int32, (16, tokens), 0)
    chosen = jnp.zeros((16, tokens), jnp.bool_)
    for head in range(H_WIDE):
        for token in range(wide_tokens):
            at = token * R_WIDE + offsets[H_MID + head]
            chosen = chosen | ((row == head * wide_tokens + token) & (position == at))
    chosen = chosen.astype(F32).astype(BF16)
    head_of = lax.broadcasted_iota(jnp.int32, (WIDE_ROWS, HEAD_DIM), 0) // wide_tokens
    blocks = []
    for a in range(4):
        both = dot(chosen, x[a, :, MID_END:], (1, 0))[:WIDE_ROWS]
        block = jnp.zeros((WIDE_ROWS, HEAD_DIM), F32)
        for head in range(H_WIDE):
            part = both[:, head * HEAD_DIM:(head + 1) * HEAD_DIM]
            block = jnp.where(head_of == head, part, block)
        blocks.append(block)
    wide[me_o, me_i] = jnp.concatenate(blocks, axis=0).astype(BF16)

    def line_copy(step, source):
        return pltpu.make_async_remote_copy(
            src_ref=wide.at[me_o, me_i], dst_ref=wide.at[me_o, source],
            send_sem=line_send.at[step], recv_sem=line_recv.at[source],
            device_id=(me_o, inner_peer(step)), device_id_type=MESH,
        )

    for step in range(1, n_inner):
        line_copy(step, me_i).start()

    for step in range(2, H_MID):
        pick_head(step)
        send_head(step)

    for copy in loads[H_MID + 1]:
        copy.wait()

    def near_head(head):
        columns = slice(head * HEAD_DIM, (head + 1) * HEAD_DIM)
        q, k, v, g = [x[a, :, columns] for a in range(4)]
        weights, score_grads = attention_parts(q, k, v, g)
        y[0, :, columns] = dot(score_grads, k, (1, 0)).astype(BF16)
        y[1, :, columns] = dot(score_grads, q, (0, 0)).astype(BF16)
        y[2, :, columns] = dot(weights, g, (0, 0)).astype(BF16)

    for head in range(H_NEAR // 2):
        near_head(head)

    for step in range(1, n_inner):
        line_copy(step, inner_peer(step)).wait_recv()

    def plane_copy(step, source):
        return pltpu.make_async_remote_copy(
            src_ref=wide.at[me_o], dst_ref=wide.at[source],
            send_sem=plane_send.at[step], recv_sem=plane_recv.at[source],
            device_id=(outer_peer(step), me_i), device_id_type=MESH,
        )

    for step in range(1, n_outer):
        plane_copy(step, me_o).start()

    def back_copy(slot, head, source):
        return pltpu.make_async_remote_copy(
            src_ref=result.at[slot, source], dst_ref=returned.at[head],
            send_sem=back_send.at[slot, source], recv_sem=back_recv.at[head],
            device_id=(me_o, source), device_id_type=MESH,
        )

    def owned(slot):
        if slot == 0:
            return me_i
        shift = lax.rem(me_i + 2 * n_inner - n_inner // 2 + lax.rem(me_o, 2), n_inner)
        return slot * n_inner + shift

    segment = n_inner * rows
    for slot in range(slots):
        head = owned(slot)

        @pl.when(head < H_MID)
        def _():
            for step in range(1, n_inner):
                source = inner_peer(step)
                mid_copy(0, slot, source, source).wait_recv()
            q, k, v, g = [arrived[slot, :, a].reshape(segment, HEAD_DIM) for a in range(4)]
            weights, score_grads = attention_parts(q, k, v, g)
            grads = (
                dot(score_grads, k, (1, 0)), dot(score_grads, q, (0, 0)), dot(weights, g, (0, 0))
            )
            for which in range(3):
                result[slot, :, which] = grads[which].astype(BF16).reshape(n_inner, rows, HEAD_DIM)
            for step in range(1, n_inner):
                back_copy(slot, head, inner_peer(step)).start()
            returned[head] = result[slot, me_i]

    for head in range(H_NEAR // 2, H_NEAR):
        near_head(head)

    def store(group, span):
        return [
            pltpu.make_async_copy(y.at[which, :, span], outputs[which].at[:, span], out_sem.at[group, which])
            for which in range(3)
        ]

    stores = store(H_MID, near_span)
    for copy in stores:
        copy.start()

    for step in range(1, n_outer):
        plane_copy(step, outer_peer(step)).wait_recv()
    devices = n_outer * n_inner
    total = devices * WIDE_ROWS
    tile = min(total, 256)

    def gathered(a, start, count):
        block = wide[...].reshape(devices, 4 * WIDE_ROWS, HEAD_DIM).astype(F32)
        return block[start:start + count, a * WIDE_ROWS:(a + 1) * WIDE_ROWS].reshape(
            count * WIDE_ROWS, HEAD_DIM).astype(BF16)

    wide_k, wide_v = gathered(1, 0, devices), gathered(2, 0, devices)
    wide_result[...] = jnp.zeros_like(wide_result)
    for first in range(0, total, tile):
        q = gathered(0, first // WIDE_ROWS, tile // WIDE_ROWS)
        g = gathered(3, first // WIDE_ROWS, tile // WIDE_ROWS)
        query_head = lax.rem(lax.broadcasted_iota(jnp.int32, (tile, total), 0), WIDE_ROWS) // wide_tokens
        key_head = lax.rem(lax.broadcasted_iota(jnp.int32, (tile, total), 1), WIDE_ROWS) // wide_tokens
        weights, score_grads = attention_parts(q, wide_k, wide_v, g, query_head == key_head)
        wide_result[0, first:first + tile] = dot(score_grads, wide_k, (1, 0))
        wide_result[1] += dot(score_grads, q, (0, 0))
        wide_result[2] += dot(weights, g, (0, 0))
    mine = pl.ds(pl.multiple_of((me_o * n_inner + me_i) * WIDE_ROWS, WIDE_ROWS), WIDE_ROWS)
    place = lax.broadcasted_iota(jnp.int32, (tokens, HEAD_DIM), 0)
    for which in range(3):
        block = wide_result[which, mine, :]
        for head in range(H_WIDE):
            spread = jnp.zeros((tokens, HEAD_DIM), F32)
            for token in range(wide_tokens):
                at = head * wide_tokens + token
                spread = jnp.where(
                    place == token * R_WIDE + offsets[H_MID + head], block[at:at + 1], spread
                )
            first = MID_END + head * HEAD_DIM
            y[which, :, first:first + HEAD_DIM] = spread.astype(BF16)

    stores += store(H_MID + 1, wide_span)
    for copy in stores[-3:]:
        copy.start()

    spread_row = lax.broadcasted_iota(jnp.int32, (tokens, rows), 1)
    spread_position = lax.broadcasted_iota(jnp.int32, (tokens, rows), 0)
    for head in range(H_MID):
        target = owner(head)

        @pl.when(me_i != target)
        def _():
            back_copy(0, head, target).wait_recv()

        place = (spread_position == spread_row * R_MID + offsets[head]).astype(F32).astype(BF16)
        columns = pl.ds(NEAR_END + head * HEAD_DIM, HEAD_DIM)
        for which in range(3):
            y[which, :, columns] = dot(place, returned[head, which], (1, 0)).astype(BF16)
        stores += store(head, columns)
        for copy in stores[-3:]:
            copy.start()

    for step in range(1, n_inner):
        line_copy(step, me_i).wait_send()
    for step in range(1, n_outer):
        plane_copy(step, me_o).wait_send()
    for head in range(H_MID):
        target = owner(head)

        @pl.when(me_i != target)
        def _():
            mid_copy(head, 0, me_i, target).wait_send()

    for slot in range(slots):
        head = owned(slot)

        @pl.when(head < H_MID)
        def _():
            for step in range(1, n_inner):
                back_copy(slot, head, inner_peer(step)).wait_send()

    for copy in stores:
        copy.wait()


def write_out(grads):
    pieces = 4

    def copies(*refs):
        sems = refs[6]
        step = refs[0].shape[0] // pieces
        started = []
        for which in range(3):
            for piece in range(pieces):
                part = pl.ds(piece * step, step)
                copy = pltpu.make_async_copy(
                    refs[which].at[part], refs[3 + which].at[part], sems.at[which, piece]
                )
                copy.start()
                started.append(copy)
        for copy in started:
            copy.wait()

    return tuple(pl.pallas_call(
        copies,
        out_shape=[jax.ShapeDtypeStruct(grad.shape, grad.dtype) for grad in grads],
        in_specs=[pl.BlockSpec(memory_space=pl.ANY)] * 3,
        out_specs=[pl.BlockSpec(memory_space=pltpu.HBM)] * 3,
        scratch_shapes=[pltpu.SemaphoreType.DMA((3, pieces))],
    )(*grads))


def body(n_outer, n_inner, queries, key_rows, values, out_grads, offsets):
    tokens, columns = queries.shape
    rows = tokens // R_MID
    slots = -(-H_MID // n_inner)
    anywhere = pl.BlockSpec(memory_space=pl.ANY)
    dma = pltpu.SemaphoreType.DMA
    grads = pl.pallas_call(
        functools.partial(kernel, n_outer, n_inner),
        out_shape=[jax.ShapeDtypeStruct((tokens, columns), BF16)] * 3,
        in_specs=[pl.BlockSpec(memory_space=pltpu.HBM)] * 5,
        out_specs=[anywhere] * 3,
        scratch_shapes=[
            pltpu.SMEM(offsets.shape, jnp.int32),
            pltpu.VMEM((4, tokens, columns), BF16),
            pltpu.VMEM((3, tokens, columns), BF16),
            pltpu.VMEM((H_MID, 4, rows, HEAD_DIM), BF16),
            pltpu.VMEM((slots, n_inner, 4, rows, HEAD_DIM), BF16),
            pltpu.VMEM((slots, n_inner, 3, rows, HEAD_DIM), BF16),
            pltpu.VMEM((H_MID, 3, rows, HEAD_DIM), BF16),
            pltpu.VMEM((n_outer, n_inner, 4 * WIDE_ROWS, HEAD_DIM), BF16),
            pltpu.VMEM((3, n_outer * n_inner * WIDE_ROWS, HEAD_DIM), F32),
            dma,
            dma((H_MID + 2, 4)),
            dma((H_MID + 2, 3)),
            dma((H_MID,)),
            dma((slots, n_inner)),
            dma((slots, n_inner)),
            dma((H_MID,)),
            dma((n_inner,)),
            dma((n_inner,)),
            dma((n_outer,)),
            dma((n_outer,)),
        ],
        compiler_params=pltpu.CompilerParams(
            collective_id=0, has_side_effects=True, vmem_limit_bytes=48 * 1024 * 1024
        ),
    )(*[pltpu.with_memory_space_constraint(a, pltpu.HBM) for a in (offsets, queries, key_rows, values, out_grads)])
    return write_out(grads)


def solution(mesh):
    split = P(("outer", "inner"), None)
    return jax.shard_map(
        functools.partial(body, mesh.shape["outer"], mesh.shape["inner"]),
        mesh=mesh,
        in_specs=(split, split, split, split, P()),
        out_specs=(split,) * 3,
        check_vma=False,
    )
```

```python
import functools
import math

import jax
import jax.numpy as jnp
from jax import lax
from jax.experimental import pallas as pl
from jax.experimental.pallas import tpu as pltpu
from jax.sharding import PartitionSpec as P

HEAD_DIM = 128
H_NEAR = 4
H_MID = 5
H_WIDE = 3
HEADS = H_NEAR + H_MID + H_WIDE
R_MID = 4
R_WIDE = 128
NEAR_END = H_NEAR * HEAD_DIM
MID_END = NEAR_END + H_MID * HEAD_DIM
WIDE_ROWS = 8
MESH = pl.DeviceIdType.MESH
F32 = jnp.float32
BF16 = jnp.bfloat16


def dot(left, right, contract):
    return lax.dot_general(left, right, ((contract[:1], contract[1:]), ((), ())), preferred_element_type=F32)


def attention_parts(q, k, v, g, mask=None):
    scale = 1.0 / math.sqrt(HEAD_DIM)
    scores = dot(q, k, (1, 1)) * scale
    if mask is not None:
        scores = jnp.where(mask, scores, -1e30)
    exponent = jnp.exp(scores - jnp.max(scores, axis=1, keepdims=True))
    weights = exponent * (1.0 / jnp.sum(exponent, axis=1, keepdims=True))
    dots = dot(g, v, (1, 1))
    row_dots = jnp.sum(weights * dots, axis=1, keepdims=True)
    score_grads = (weights * (dots - row_dots) * scale).astype(BF16)
    return weights.astype(BF16), score_grads


def kernel(
    n_outer, n_inner, offsets_in, queries, key_rows, values, out_grads, grad_q, grad_k, grad_v,
    offsets, x, picked, arrived, result, returned, wide, wide_result,
    offsets_sem, in_sem, mid_send, mid_recv, back_send, back_recv,
    line_send, line_recv, plane_send, plane_recv,
):
    tokens = x.shape[1]
    rows = tokens // R_MID
    wide_tokens = tokens // R_WIDE
    slots = arrived.shape[0]
    me_o, me_i = lax.axis_index("outer"), lax.axis_index("inner")
    inputs = (queries, key_rows, values, out_grads)
    outputs = (grad_q, grad_k, grad_v)

    def inner_peer(step):
        return lax.rem(me_i + step, n_inner)

    def outer_peer(step):
        return lax.rem(me_o + step, n_outer)

    barrier = pltpu.get_barrier_semaphore()
    for step in range(1, n_inner):
        pl.semaphore_signal(barrier, inc=1, device_id=(me_o, inner_peer(step)), device_id_type=MESH)
    for step in range(1, n_outer):
        pl.semaphore_signal(barrier, inc=1, device_id=(outer_peer(step), me_i), device_id_type=MESH)

    first_head = jnp.where(me_i < n_inner // 2, (H_MID - 1) // 2, 0)

    def head_at(step):
        if step == 0:
            return jnp.int32(H_MID - 1)
        return lax.rem(first_head + step - 1, H_MID - 1)

    def head_columns(head):
        return pl.ds(pl.multiple_of(NEAR_END + head * HEAD_DIM, HEAD_DIM), HEAD_DIM)

    def load(group, span):
        return [
            pltpu.make_async_copy(inputs[a].at[:, span], x.at[a, :, span], in_sem.at[group, a])
            for a in range(4)
        ]

    near_span, wide_span = pl.ds(0, NEAR_END), pl.ds(MID_END, H_WIDE * HEAD_DIM)
    offsets_load = pltpu.make_async_copy(offsets_in, offsets, offsets_sem)
    offsets_load.start()
    loads = [load(step, head_columns(head_at(step))) for step in range(H_MID)]
    loads += [load(H_MID, wide_span), load(H_MID + 1, near_span)]
    for group in (0, 1, H_MID, *range(2, H_MID), H_MID + 1):
        for copy in loads[group]:
            copy.start()

    def owner(head):
        turned = head + n_inner // 2 + n_inner - lax.rem(me_o, 2)
        return jnp.where(head < n_inner, head, lax.rem(turned, n_inner))

    def mid_copy(head, slot, source, target):
        return pltpu.make_async_remote_copy(
            src_ref=picked.at[head], dst_ref=arrived.at[slot, source],
            send_sem=mid_send.at[head], recv_sem=mid_recv.at[slot, source],
            device_id=(me_o, target), device_id_type=MESH,
        )

    pick_row = lax.broadcasted_iota(jnp.int32, (rows, tokens), 0)
    pick_position = lax.broadcasted_iota(jnp.int32, (rows, tokens), 1)

    def pick_head(step):
        for copy in loads[step]:
            copy.wait()
        head = head_at(step)
        pick = (pick_position == pick_row * R_MID + offsets[head]).astype(F32).astype(BF16)
        for a in range(4):
            picked[head, a] = dot(pick, x[a, :, head_columns(head)], (1, 0)).astype(BF16)

    def send_head(step):
        head = head_at(step)
        target, slot = owner(head), head // n_inner

        @pl.when(me_i != target)
        def _():
            mid_copy(head, slot, me_i, target).start()

        @pl.when(me_i == target)
        def _():
            arrived[slot, me_i] = picked[head]

    offsets_load.wait()
    pick_head(0)
    pl.semaphore_wait(barrier, n_inner - 1 + n_outer - 1)
    send_head(0)
    pick_head(1)
    send_head(1)

    for copy in loads[H_MID]:
        copy.wait()
    position = lax.broadcasted_iota(jnp.int32, (16, tokens), 1)
    row = lax.broadcasted_iota(jnp.int32, (16, tokens), 0)
    chosen = jnp.zeros((16, tokens), jnp.bool_)
    for head in range(H_WIDE):
        for token in range(wide_tokens):
            at = token * R_WIDE + offsets[H_MID + head]
            chosen = chosen | ((row == head * wide_tokens + token) & (position == at))
    chosen = chosen.astype(F32).astype(BF16)
    head_of = lax.broadcasted_iota(jnp.int32, (WIDE_ROWS, HEAD_DIM), 0) // wide_tokens
    blocks = []
    for a in range(4):
        both = dot(chosen, x[a, :, MID_END:], (1, 0))[:WIDE_ROWS]
        block = jnp.zeros((WIDE_ROWS, HEAD_DIM), F32)
        for head in range(H_WIDE):
            part = both[:, head * HEAD_DIM:(head + 1) * HEAD_DIM]
            block = jnp.where(head_of == head, part, block)
        blocks.append(block)
    wide[me_o, me_i] = jnp.concatenate(blocks, axis=0).astype(BF16)

    def line_copy(step, source):
        return pltpu.make_async_remote_copy(
            src_ref=wide.at[me_o, me_i], dst_ref=wide.at[me_o, source],
            send_sem=line_send.at[step], recv_sem=line_recv.at[source],
            device_id=(me_o, inner_peer(step)), device_id_type=MESH,
        )

    for step in range(1, n_inner):
        line_copy(step, me_i).start()

    for step in range(2, H_MID):
        pick_head(step)
        send_head(step)

    for copy in loads[H_MID + 1]:
        copy.wait()

    def near_head(head):
        columns = slice(head * HEAD_DIM, (head + 1) * HEAD_DIM)
        q, k, v, g = [x[a, :, columns] for a in range(4)]
        weights, score_grads = attention_parts(q, k, v, g)
        outputs[0][:, columns] = dot(score_grads, k, (1, 0)).astype(BF16)
        outputs[1][:, columns] = dot(score_grads, q, (0, 0)).astype(BF16)
        outputs[2][:, columns] = dot(weights, g, (0, 0)).astype(BF16)

    for head in range(H_NEAR // 2):
        near_head(head)

    for step in range(1, n_inner):
        line_copy(step, inner_peer(step)).wait_recv()

    def plane_copy(step, source):
        return pltpu.make_async_remote_copy(
            src_ref=wide.at[me_o], dst_ref=wide.at[source],
            send_sem=plane_send.at[step], recv_sem=plane_recv.at[source],
            device_id=(outer_peer(step), me_i), device_id_type=MESH,
        )

    for step in range(1, n_outer):
        plane_copy(step, me_o).start()

    def back_copy(slot, head, source, which):
        return pltpu.make_async_remote_copy(
            src_ref=result.at[slot, source, which], dst_ref=returned.at[head, which],
            send_sem=back_send.at[slot, source, which], recv_sem=back_recv.at[head, which],
            device_id=(me_o, source), device_id_type=MESH,
        )

    def owned(slot):
        if slot == 0:
            return me_i
        shift = lax.rem(me_i + 2 * n_inner - n_inner // 2 + lax.rem(me_o, 2), n_inner)
        return slot * n_inner + shift

    segment = n_inner * rows
    for slot in reversed(range(slots)):
        head = owned(slot)

        @pl.when(head < H_MID)
        def _():
            for step in range(1, n_inner):
                source = inner_peer(step)
                mid_copy(0, slot, source, source).wait_recv()
            q, k, v, g = [arrived[slot, :, a].reshape(segment, HEAD_DIM) for a in range(4)]
            weights, score_grads = attention_parts(q, k, v, g)
            for which, left, right, contract in (
                (2, weights, g, (0, 0)), (0, score_grads, k, (1, 0)), (1, score_grads, q, (0, 0))
            ):
                grads = dot(left, right, contract).astype(BF16)
                result[slot, :, which] = grads.reshape(n_inner, rows, HEAD_DIM)
                for step in range(1, n_inner):
                    back_copy(slot, head, inner_peer(step), which).start()
                returned[head, which] = result[slot, me_i, which]

    for head in range(H_NEAR // 2, H_NEAR):
        near_head(head)

    for step in range(1, n_outer):
        plane_copy(step, outer_peer(step)).wait_recv()
    devices = n_outer * n_inner
    total = devices * WIDE_ROWS
    tile = min(total, 256)

    def gathered(a, start, count):
        block = wide[...].reshape(devices, 4 * WIDE_ROWS, HEAD_DIM).astype(F32)
        return block[start:start + count, a * WIDE_ROWS:(a + 1) * WIDE_ROWS].reshape(
            count * WIDE_ROWS, HEAD_DIM).astype(BF16)

    wide_k, wide_v = gathered(1, 0, devices), gathered(2, 0, devices)
    wide_result[...] = jnp.zeros_like(wide_result)
    for first in range(0, total, tile):
        q = gathered(0, first // WIDE_ROWS, tile // WIDE_ROWS)
        g = gathered(3, first // WIDE_ROWS, tile // WIDE_ROWS)
        query_head = lax.rem(lax.broadcasted_iota(jnp.int32, (tile, total), 0), WIDE_ROWS) // wide_tokens
        key_head = lax.rem(lax.broadcasted_iota(jnp.int32, (tile, total), 1), WIDE_ROWS) // wide_tokens
        weights, score_grads = attention_parts(q, wide_k, wide_v, g, query_head == key_head)
        wide_result[0, first:first + tile] = dot(score_grads, wide_k, (1, 0))
        wide_result[1] += dot(score_grads, q, (0, 0))
        wide_result[2] += dot(weights, g, (0, 0))
    mine = pl.ds(pl.multiple_of((me_o * n_inner + me_i) * WIDE_ROWS, WIDE_ROWS), WIDE_ROWS)
    place = lax.broadcasted_iota(jnp.int32, (tokens, HEAD_DIM), 0)
    for which in range(3):
        block = wide_result[which, mine, :]
        for head in range(H_WIDE):
            spread = jnp.zeros((tokens, HEAD_DIM), F32)
            for token in range(wide_tokens):
                at = head * wide_tokens + token
                spread = jnp.where(
                    place == token * R_WIDE + offsets[H_MID + head], block[at:at + 1], spread
                )
            first = MID_END + head * HEAD_DIM
            outputs[which][:, first:first + HEAD_DIM] = spread.astype(BF16)

    spread_row = lax.broadcasted_iota(jnp.int32, (tokens, rows), 1)
    spread_position = lax.broadcasted_iota(jnp.int32, (tokens, rows), 0)
    for head in range(H_MID):
        target = owner(head)
        place = (spread_position == spread_row * R_MID + offsets[head]).astype(F32).astype(BF16)
        columns = slice(NEAR_END + head * HEAD_DIM, NEAR_END + (head + 1) * HEAD_DIM)
        for which in (2, 0, 1):

            @pl.when(me_i != target)
            def _():
                back_copy(0, head, target, which).wait_recv()

            outputs[which][:, columns] = dot(place, returned[head, which], (1, 0)).astype(BF16)

    for step in range(1, n_inner):
        line_copy(step, me_i).wait_send()
    for step in range(1, n_outer):
        plane_copy(step, me_o).wait_send()
    for head in range(H_MID):
        target = owner(head)

        @pl.when(me_i != target)
        def _():
            mid_copy(head, 0, me_i, target).wait_send()

    for slot in range(slots):
        head = owned(slot)

        @pl.when(head < H_MID)
        def _():
            for step in range(1, n_inner):
                for which in range(3):
                    back_copy(slot, head, inner_peer(step), which).wait_send()


def write_out(grads):
    pieces = 4

    def copies(*refs):
        sems = refs[6]
        step = refs[0].shape[0] // pieces
        started = []
        for which in range(3):
            for piece in range(pieces):
                part = pl.ds(piece * step, step)
                copy = pltpu.make_async_copy(
                    refs[which].at[part], refs[3 + which].at[part], sems.at[which, piece]
                )
                copy.start()
                started.append(copy)
        for copy in started:
            copy.wait()

    return tuple(pl.pallas_call(
        copies,
        out_shape=[jax.ShapeDtypeStruct(grad.shape, grad.dtype) for grad in grads],
        in_specs=[pl.BlockSpec(memory_space=pltpu.VMEM)] * 3,
        out_specs=[pl.BlockSpec(memory_space=pltpu.HBM)] * 3,
        scratch_shapes=[pltpu.SemaphoreType.DMA((3, pieces))],
        compiler_params=pltpu.CompilerParams(vmem_limit_bytes=16 * 1024 * 1024),
    )(*[pltpu.with_memory_space_constraint(grad, pltpu.VMEM) for grad in grads]))


def body(n_outer, n_inner, queries, key_rows, values, out_grads, offsets):
    tokens, columns = queries.shape
    rows = tokens // R_MID
    slots = -(-H_MID // n_inner)
    dma = pltpu.SemaphoreType.DMA
    grads = pl.pallas_call(
        functools.partial(kernel, n_outer, n_inner),
        out_shape=[jax.ShapeDtypeStruct((tokens, columns), BF16)] * 3,
        in_specs=[pl.BlockSpec(memory_space=pltpu.HBM)] * 5,
        out_specs=[pl.BlockSpec(memory_space=pltpu.VMEM)] * 3,
        scratch_shapes=[
            pltpu.SMEM(offsets.shape, jnp.int32),
            pltpu.VMEM((4, tokens, columns), BF16),
            pltpu.VMEM((H_MID, 4, rows, HEAD_DIM), BF16),
            pltpu.VMEM((slots, n_inner, 4, rows, HEAD_DIM), BF16),
            pltpu.VMEM((slots, n_inner, 3, rows, HEAD_DIM), BF16),
            pltpu.VMEM((H_MID, 3, rows, HEAD_DIM), BF16),
            pltpu.VMEM((n_outer, n_inner, 4 * WIDE_ROWS, HEAD_DIM), BF16),
            pltpu.VMEM((3, n_outer * n_inner * WIDE_ROWS, HEAD_DIM), F32),
            dma,
            dma((H_MID + 2, 4)),
            dma((H_MID,)),
            dma((slots, n_inner)),
            dma((slots, n_inner, 3)),
            dma((H_MID, 3)),
            dma((n_inner,)),
            dma((n_inner,)),
            dma((n_outer,)),
            dma((n_outer,)),
        ],
        compiler_params=pltpu.CompilerParams(
            collective_id=0, has_side_effects=True, vmem_limit_bytes=48 * 1024 * 1024
        ),
    )(*[pltpu.with_memory_space_constraint(a, pltpu.HBM) for a in (offsets, queries, key_rows, values, out_grads)])
    return write_out(grads)


def solution(mesh):
    split = P(("outer", "inner"), None)
    return jax.shard_map(
        functools.partial(body, mesh.shape["outer"], mesh.shape["inner"]),
        mesh=mesh,
        in_specs=(split, split, split, split, P()),
        out_specs=(split,) * 3,
        check_vma=False,
    )
```

```python
import functools
import math

import jax
import jax.numpy as jnp
from jax import lax
from jax.experimental import pallas as pl
from jax.experimental.pallas import tpu as pltpu
from jax.sharding import PartitionSpec as P

HEAD_DIM = 128
H_NEAR = 4
H_MID = 5
H_WIDE = 3
HEADS = H_NEAR + H_MID + H_WIDE
R_MID = 4
R_WIDE = 128
NEAR_END = H_NEAR * HEAD_DIM
MID_END = NEAR_END + H_MID * HEAD_DIM
WIDE_ROWS = 8
MESH = pl.DeviceIdType.MESH
F32 = jnp.float32
BF16 = jnp.bfloat16


def dot(left, right, contract):
    return lax.dot_general(left, right, ((contract[:1], contract[1:]), ((), ())), preferred_element_type=F32)


def attention_parts(q, k, v, g, mask=None):
    scale = 1.0 / math.sqrt(HEAD_DIM)
    scores = dot(k, q, (1, 1)) * scale
    if mask is not None:
        scores = jnp.where(mask, scores, -1e30)
    exponent = jnp.exp(scores - jnp.max(scores, axis=0, keepdims=True))
    weights = exponent * (1.0 / jnp.sum(exponent, axis=0, keepdims=True))
    dots = dot(v, g, (1, 1))
    row_dots = jnp.sum(weights * dots, axis=0, keepdims=True)
    score_grads = (weights * (dots - row_dots) * scale).astype(BF16)
    return weights.astype(BF16), score_grads


def kernel(
    n_outer, n_inner, offsets_in, queries, key_rows, values, out_grads, grad_q, grad_k, grad_v,
    offsets, x, picked, arrived, result, returned, wide, wide_result,
    offsets_sem, in_sem, mid_send, mid_recv, back_send, back_recv,
    line_send, line_recv, plane_send, plane_recv,
):
    tokens = x.shape[1]
    rows = tokens // R_MID
    wide_tokens = tokens // R_WIDE
    slots = arrived.shape[0]
    me_o, me_i = lax.axis_index("outer"), lax.axis_index("inner")
    inputs = (queries, key_rows, values, out_grads)
    outputs = (grad_q, grad_k, grad_v)

    def inner_peer(step):
        return lax.rem(me_i + step, n_inner)

    def outer_peer(step):
        return lax.rem(me_o + step, n_outer)

    barrier = pltpu.get_barrier_semaphore()
    for step in range(1, n_inner):
        pl.semaphore_signal(barrier, inc=1, device_id=(me_o, inner_peer(step)), device_id_type=MESH)
    for step in range(1, n_outer):
        pl.semaphore_signal(barrier, inc=1, device_id=(outer_peer(step), me_i), device_id_type=MESH)

    first_head = jnp.where(me_i < n_inner // 2, (H_MID - 1) // 2, 0)

    def head_at(step):
        if step == 0:
            return jnp.int32(H_MID - 1)
        return lax.rem(first_head + step - 1, H_MID - 1)

    def head_columns(head):
        return pl.ds(pl.multiple_of(NEAR_END + head * HEAD_DIM, HEAD_DIM), HEAD_DIM)

    def load(group, span):
        return [
            pltpu.make_async_copy(inputs[a].at[:, span], x.at[a, :, span], in_sem.at[group, a])
            for a in range(4)
        ]

    near_span, wide_span = pl.ds(0, NEAR_END), pl.ds(MID_END, H_WIDE * HEAD_DIM)
    offsets_load = pltpu.make_async_copy(offsets_in, offsets, offsets_sem)
    offsets_load.start()
    loads = [load(step, head_columns(head_at(step))) for step in range(H_MID)]
    loads += [load(H_MID, wide_span), load(H_MID + 1, near_span)]
    for group in (0, 1, H_MID, *range(2, H_MID), H_MID + 1):
        for copy in loads[group]:
            copy.start()

    def owner(head):
        turned = head + n_inner // 2 + n_inner - lax.rem(me_o, 2)
        return jnp.where(head < n_inner, head, lax.rem(turned, n_inner))

    def mid_copy(head, slot, source, target):
        return pltpu.make_async_remote_copy(
            src_ref=picked.at[head], dst_ref=arrived.at[slot, source],
            send_sem=mid_send.at[head], recv_sem=mid_recv.at[slot, source],
            device_id=(me_o, target), device_id_type=MESH,
        )

    pick_row = lax.broadcasted_iota(jnp.int32, (rows, tokens), 0)
    pick_position = lax.broadcasted_iota(jnp.int32, (rows, tokens), 1)

    def pick_head(step):
        for copy in loads[step]:
            copy.wait()
        head = head_at(step)
        pick = (pick_position == pick_row * R_MID + offsets[head]).astype(F32).astype(BF16)
        for a in range(4):
            picked[head, a] = dot(pick, x[a, :, head_columns(head)], (1, 0)).astype(BF16)

    def send_head(step):
        head = head_at(step)
        target, slot = owner(head), head // n_inner

        @pl.when(me_i != target)
        def _():
            mid_copy(head, slot, me_i, target).start()

        @pl.when(me_i == target)
        def _():
            arrived[slot, me_i] = picked[head]

    offsets_load.wait()
    pick_head(0)
    pl.semaphore_wait(barrier, n_inner - 1 + n_outer - 1)
    send_head(0)
    pick_head(1)
    send_head(1)

    for copy in loads[H_MID]:
        copy.wait()
    position = lax.broadcasted_iota(jnp.int32, (16, tokens), 1)
    row = lax.broadcasted_iota(jnp.int32, (16, tokens), 0)
    chosen = jnp.zeros((16, tokens), jnp.bool_)
    for head in range(H_WIDE):
        for token in range(wide_tokens):
            at = token * R_WIDE + offsets[H_MID + head]
            chosen = chosen | ((row == head * wide_tokens + token) & (position == at))
    chosen = chosen.astype(F32).astype(BF16)
    head_of = lax.broadcasted_iota(jnp.int32, (WIDE_ROWS, HEAD_DIM), 0) // wide_tokens
    blocks = []
    for a in range(4):
        both = dot(chosen, x[a, :, MID_END:], (1, 0))[:WIDE_ROWS]
        block = jnp.zeros((WIDE_ROWS, HEAD_DIM), F32)
        for head in range(H_WIDE):
            part = both[:, head * HEAD_DIM:(head + 1) * HEAD_DIM]
            block = jnp.where(head_of == head, part, block)
        blocks.append(block)
    wide[me_o, me_i] = jnp.concatenate(blocks, axis=0).astype(BF16)

    def line_copy(step, source):
        return pltpu.make_async_remote_copy(
            src_ref=wide.at[me_o, me_i], dst_ref=wide.at[me_o, source],
            send_sem=line_send.at[step], recv_sem=line_recv.at[source],
            device_id=(me_o, inner_peer(step)), device_id_type=MESH,
        )

    for step in range(1, n_inner):
        line_copy(step, me_i).start()

    for step in range(2, H_MID):
        pick_head(step)
        send_head(step)

    for copy in loads[H_MID + 1]:
        copy.wait()

    def near_head(head):
        columns = slice(head * HEAD_DIM, (head + 1) * HEAD_DIM)
        q, k, v, g = [x[a, :, columns] for a in range(4)]
        weights, score_grads = attention_parts(q, k, v, g)
        outputs[0][:, columns] = dot(score_grads, k, (0, 0)).astype(BF16)
        outputs[1][:, columns] = dot(score_grads, q, (1, 0)).astype(BF16)
        outputs[2][:, columns] = dot(weights, g, (1, 0)).astype(BF16)

    def back_copy(slot, head, source, which):
        return pltpu.make_async_remote_copy(
            src_ref=result.at[slot, source, which], dst_ref=returned.at[head, which],
            send_sem=back_send.at[slot, source, which], recv_sem=back_recv.at[head, which],
            device_id=(me_o, source), device_id_type=MESH,
        )

    def owned(slot):
        if slot == 0:
            return me_i
        shift = lax.rem(me_i + 2 * n_inner - n_inner // 2 + lax.rem(me_o, 2), n_inner)
        return slot * n_inner + shift

    segment = n_inner * rows
    def own_slot(slot):
        head = owned(slot)

        @pl.when(head < H_MID)
        def _():
            for step in range(1, n_inner):
                source = inner_peer(step)
                mid_copy(0, slot, source, source).wait_recv()
            q, k, v, g = [arrived[slot, :, a].reshape(segment, HEAD_DIM) for a in range(4)]
            weights, score_grads = attention_parts(q, k, v, g)
            for which, left, right, contract in (
                (2, weights, g, (1, 0)), (1, score_grads, q, (1, 0)), (0, score_grads, k, (0, 0))
            ):
                grads = dot(left, right, contract).astype(BF16)
                result[slot, :, which] = grads.reshape(n_inner, rows, HEAD_DIM)
                for step in range(1, n_inner):
                    back_copy(slot, head, inner_peer(step), which).start()
                returned[head, which] = result[slot, me_i, which]

    def first_near():
        for head in range(H_NEAR // 2):
            near_head(head)

    several = owned(slots - 1) < H_MID if slots > 1 else me_i < 0
    pl.when(jnp.logical_not(several))(first_near)
    for slot in reversed(range(1, slots)):
        own_slot(slot)

    for step in range(1, n_inner):
        line_copy(step, inner_peer(step)).wait_recv()

    def plane_copy(step, source):
        return pltpu.make_async_remote_copy(
            src_ref=wide.at[me_o], dst_ref=wide.at[source],
            send_sem=plane_send.at[step], recv_sem=plane_recv.at[source],
            device_id=(outer_peer(step), me_i), device_id_type=MESH,
        )

    for step in range(1, n_outer):
        plane_copy(step, me_o).start()

    own_slot(0)
    pl.when(several)(first_near)
    for head in range(H_NEAR // 2, H_NEAR):
        near_head(head)

    for step in range(1, n_outer):
        plane_copy(step, outer_peer(step)).wait_recv()
    devices = n_outer * n_inner
    total = devices * WIDE_ROWS
    tile = min(total, 256)

    def gathered(a, start, count):
        block = wide[...].reshape(devices, 4 * WIDE_ROWS, HEAD_DIM).astype(F32)
        return block[start:start + count, a * WIDE_ROWS:(a + 1) * WIDE_ROWS].reshape(
            count * WIDE_ROWS, HEAD_DIM).astype(BF16)

    wide_k, wide_v = gathered(1, 0, devices), gathered(2, 0, devices)
    wide_result[...] = jnp.zeros_like(wide_result)
    for first in range(0, total, tile):
        q = gathered(0, first // WIDE_ROWS, tile // WIDE_ROWS)
        g = gathered(3, first // WIDE_ROWS, tile // WIDE_ROWS)
        key_head = lax.rem(lax.broadcasted_iota(jnp.int32, (total, 1), 0), WIDE_ROWS) // wide_tokens
        query_head = lax.rem(lax.broadcasted_iota(jnp.int32, (1, tile), 1), WIDE_ROWS) // wide_tokens
        weights, score_grads = attention_parts(q, wide_k, wide_v, g, key_head == query_head)
        wide_result[0, first:first + tile] = dot(score_grads, wide_k, (0, 0))
        wide_result[1] += dot(score_grads, q, (1, 0))
        wide_result[2] += dot(weights, g, (1, 0))
    mine = pl.ds(pl.multiple_of((me_o * n_inner + me_i) * WIDE_ROWS, WIDE_ROWS), WIDE_ROWS)
    place = lax.broadcasted_iota(jnp.int32, (tokens, HEAD_DIM), 0)
    for which in range(3):
        block = wide_result[which, mine, :]
        for head in range(H_WIDE):
            spread = jnp.zeros((tokens, HEAD_DIM), F32)
            for token in range(wide_tokens):
                at = head * wide_tokens + token
                spread = jnp.where(
                    place == token * R_WIDE + offsets[H_MID + head], block[at:at + 1], spread
                )
            first = MID_END + head * HEAD_DIM
            outputs[which][:, first:first + HEAD_DIM] = spread.astype(BF16)

    spread_row = lax.broadcasted_iota(jnp.int32, (tokens, rows), 1)
    spread_position = lax.broadcasted_iota(jnp.int32, (tokens, rows), 0)
    returning = [lax.rem(me_i + step, H_MID - 1) for step in (0, 1, 3, 2)]
    for head in (returning[0], jnp.int32(H_MID - 1), *returning[1:]):
        target = owner(head)
        place = (spread_position == spread_row * R_MID + offsets[head]).astype(F32).astype(BF16)
        columns = head_columns(head)
        for which in (2, 1, 0):

            @pl.when(me_i != target)
            def _():
                back_copy(0, head, target, which).wait_recv()

            outputs[which][:, columns] = dot(place, returned[head, which], (1, 0)).astype(BF16)

    for step in range(1, n_inner):
        line_copy(step, me_i).wait_send()
    for step in range(1, n_outer):
        plane_copy(step, me_o).wait_send()
    for head in range(H_MID):
        target = owner(head)

        @pl.when(me_i != target)
        def _():
            mid_copy(head, 0, me_i, target).wait_send()

    for slot in range(slots):
        head = owned(slot)

        @pl.when(head < H_MID)
        def _():
            for step in range(1, n_inner):
                for which in range(3):
                    back_copy(slot, head, inner_peer(step), which).wait_send()


def write_out(grads):
    pieces = 4

    def copies(*refs):
        sems = refs[6]
        step = refs[0].shape[0] // pieces
        started = []
        for which in range(3):
            for piece in range(pieces):
                part = pl.ds(piece * step, step)
                copy = pltpu.make_async_copy(
                    refs[which].at[part], refs[3 + which].at[part], sems.at[which, piece]
                )
                copy.start()
                started.append(copy)
        for copy in started:
            copy.wait()

    return tuple(pl.pallas_call(
        copies,
        out_shape=[jax.ShapeDtypeStruct(grad.shape, grad.dtype) for grad in grads],
        in_specs=[pl.BlockSpec(memory_space=pltpu.VMEM)] * 3,
        out_specs=[pl.BlockSpec(memory_space=pltpu.HBM)] * 3,
        scratch_shapes=[pltpu.SemaphoreType.DMA((3, pieces))],
        compiler_params=pltpu.CompilerParams(vmem_limit_bytes=16 * 1024 * 1024),
    )(*[pltpu.with_memory_space_constraint(grad, pltpu.VMEM) for grad in grads]))


def body(n_outer, n_inner, queries, key_rows, values, out_grads, offsets):
    tokens, columns = queries.shape
    rows = tokens // R_MID
    slots = -(-H_MID // n_inner)
    dma = pltpu.SemaphoreType.DMA
    grads = pl.pallas_call(
        functools.partial(kernel, n_outer, n_inner),
        out_shape=[jax.ShapeDtypeStruct((tokens, columns), BF16)] * 3,
        in_specs=[pl.BlockSpec(memory_space=pltpu.HBM)] * 5,
        out_specs=[pl.BlockSpec(memory_space=pltpu.VMEM)] * 3,
        scratch_shapes=[
            pltpu.SMEM(offsets.shape, jnp.int32),
            pltpu.VMEM((4, tokens, columns), BF16),
            pltpu.VMEM((H_MID, 4, rows, HEAD_DIM), BF16),
            pltpu.VMEM((slots, n_inner, 4, rows, HEAD_DIM), BF16),
            pltpu.VMEM((slots, n_inner, 3, rows, HEAD_DIM), BF16),
            pltpu.VMEM((H_MID, 3, rows, HEAD_DIM), BF16),
            pltpu.VMEM((n_outer, n_inner, 4 * WIDE_ROWS, HEAD_DIM), BF16),
            pltpu.VMEM((3, n_outer * n_inner * WIDE_ROWS, HEAD_DIM), F32),
            dma,
            dma((H_MID + 2, 4)),
            dma((H_MID,)),
            dma((slots, n_inner)),
            dma((slots, n_inner, 3)),
            dma((H_MID, 3)),
            dma((n_inner,)),
            dma((n_inner,)),
            dma((n_outer,)),
            dma((n_outer,)),
        ],
        compiler_params=pltpu.CompilerParams(
            collective_id=0, has_side_effects=True, vmem_limit_bytes=48 * 1024 * 1024
        ),
    )(*[pltpu.with_memory_space_constraint(a, pltpu.HBM) for a in (offsets, queries, key_rows, values, out_grads)])
    return write_out(grads)


def solution(mesh):
    split = P(("outer", "inner"), None)
    return jax.shard_map(
        functools.partial(body, mesh.shape["outer"], mesh.shape["inner"]),
        mesh=mesh,
        in_specs=(split, split, split, split, P()),
        out_specs=(split,) * 3,
        check_vma=False,
    )
```

```python
import functools
import math

import jax
import jax.numpy as jnp
from jax import lax
from jax.experimental import pallas as pl
from jax.experimental.pallas import tpu as pltpu
from jax.sharding import PartitionSpec as P

HEAD_DIM = 128
H_NEAR = 4
H_MID = 5
H_WIDE = 3
HEADS = H_NEAR + H_MID + H_WIDE
R_MID = 4
R_WIDE = 128
NEAR_END = H_NEAR * HEAD_DIM
MID_END = NEAR_END + H_MID * HEAD_DIM
WIDE_ROWS = 8
MESH = pl.DeviceIdType.MESH
F32 = jnp.float32
BF16 = jnp.bfloat16


def dot(left, right, contract):
    return lax.dot_general(left, right, ((contract[:1], contract[1:]), ((), ())), preferred_element_type=F32)


def attention_parts(q, k, v, g, mask=None):
    scale = 1.0 / math.sqrt(HEAD_DIM)
    scores = dot(k, q, (1, 1)) * scale
    if mask is not None:
        scores = jnp.where(mask, scores, -1e30)
    exponent = jnp.exp(scores - jnp.max(scores, axis=0, keepdims=True))
    weights = exponent * (1.0 / jnp.sum(exponent, axis=0, keepdims=True))
    dots = dot(v, g, (1, 1))
    row_dots = jnp.sum(weights * dots, axis=0, keepdims=True)
    score_grads = (weights * (dots - row_dots) * scale).astype(BF16)
    return weights.astype(BF16), score_grads


def kernel(
    n_outer, n_inner, offsets_in, queries, key_rows, values, out_grads, grad_q, grad_k, grad_v,
    offsets, x, picked, arrived, result, returned, wide, wide_result,
    offsets_sem, in_sem, mid_send, mid_recv, back_send, back_recv,
    line_send, line_recv, plane_send, plane_recv,
):
    tokens = x.shape[1]
    rows = tokens // R_MID
    wide_tokens = tokens // R_WIDE
    slots = arrived.shape[0]
    me_o, me_i = lax.axis_index("outer"), lax.axis_index("inner")
    inputs = (queries, key_rows, values, out_grads)
    outputs = (grad_q, grad_k, grad_v)

    def inner_peer(step):
        return lax.rem(me_i + step, n_inner)

    def outer_peer(step):
        return lax.rem(me_o + step, n_outer)

    barrier = pltpu.get_barrier_semaphore()
    for step in range(1, n_inner):
        pl.semaphore_signal(barrier, inc=1, device_id=(me_o, inner_peer(step)), device_id_type=MESH)
    for step in range(1, n_outer):
        pl.semaphore_signal(barrier, inc=1, device_id=(outer_peer(step), me_i), device_id_type=MESH)

    left = me_i < n_inner // 2
    half = (H_MID - 1) // 2

    def head_at(step):
        if step == 0:
            return jnp.int32(H_MID - 1)
        return jnp.where(
            left, lax.rem(half + step - 1, H_MID - 1), lax.rem(half + H_MID - 1 - step, H_MID - 1)
        )

    def head_columns(head):
        return pl.ds(pl.multiple_of(NEAR_END + head * HEAD_DIM, HEAD_DIM), HEAD_DIM)

    def load(group, span):
        return [
            pltpu.make_async_copy(inputs[a].at[:, span], x.at[a, :, span], in_sem.at[group, a])
            for a in range(4)
        ]

    near_span, wide_span = pl.ds(0, NEAR_END), pl.ds(MID_END, H_WIDE * HEAD_DIM)
    offsets_load = pltpu.make_async_copy(offsets_in, offsets, offsets_sem)
    offsets_load.start()
    loads = [load(step, head_columns(head_at(step))) for step in range(H_MID)]
    loads += [load(H_MID, wide_span), load(H_MID + 1, near_span)]
    for group in range(H_MID + 2):
        for copy in loads[group]:
            copy.start()

    def owner(head):
        turned = head + n_inner // 2 + n_inner - lax.rem(me_o, 2)
        return jnp.where(head < n_inner, head, lax.rem(turned, n_inner))

    def mid_copy(head, slot, source, target):
        return pltpu.make_async_remote_copy(
            src_ref=picked.at[head], dst_ref=arrived.at[slot, source],
            send_sem=mid_send.at[head], recv_sem=mid_recv.at[slot, source],
            device_id=(me_o, target), device_id_type=MESH,
        )

    pick_row = lax.broadcasted_iota(jnp.int32, (rows, tokens), 0)
    pick_position = lax.broadcasted_iota(jnp.int32, (rows, tokens), 1)

    def pick_head(step):
        for copy in loads[step]:
            copy.wait()
        head = head_at(step)
        pick = (pick_position == pick_row * R_MID + offsets[head]).astype(F32).astype(BF16)
        for a in range(4):
            picked[head, a] = dot(pick, x[a, :, head_columns(head)], (1, 0)).astype(BF16)

    def send_head(step):
        head = head_at(step)
        target, slot = owner(head), head // n_inner

        @pl.when(me_i != target)
        def _():
            mid_copy(head, slot, me_i, target).start()

        @pl.when(me_i == target)
        def _():
            arrived[slot, me_i] = picked[head]

    offsets_load.wait()
    pick_head(0)
    pl.semaphore_wait(barrier, n_inner - 1 + n_outer - 1)
    send_head(0)
    pick_head(1)
    send_head(1)

    for step in range(2, H_MID):
        pick_head(step)
        send_head(step)

    for copy in loads[H_MID]:
        copy.wait()
    position = lax.broadcasted_iota(jnp.int32, (16, tokens), 1)
    row = lax.broadcasted_iota(jnp.int32, (16, tokens), 0)
    chosen = jnp.zeros((16, tokens), jnp.bool_)
    for head in range(H_WIDE):
        for token in range(wide_tokens):
            at = token * R_WIDE + offsets[H_MID + head]
            chosen = chosen | ((row == head * wide_tokens + token) & (position == at))
    chosen = chosen.astype(F32).astype(BF16)
    head_of = lax.broadcasted_iota(jnp.int32, (WIDE_ROWS, HEAD_DIM), 0) // wide_tokens
    blocks = []
    for a in range(4):
        both = dot(chosen, x[a, :, MID_END:], (1, 0))[:WIDE_ROWS]
        block = jnp.zeros((WIDE_ROWS, HEAD_DIM), F32)
        for head in range(H_WIDE):
            part = both[:, head * HEAD_DIM:(head + 1) * HEAD_DIM]
            block = jnp.where(head_of == head, part, block)
        blocks.append(block)
    wide[me_o, me_i] = jnp.concatenate(blocks, axis=0).astype(BF16)

    def line_copy(step, source):
        return pltpu.make_async_remote_copy(
            src_ref=wide.at[me_o, me_i], dst_ref=wide.at[me_o, source],
            send_sem=line_send.at[step], recv_sem=line_recv.at[source],
            device_id=(me_o, inner_peer(step)), device_id_type=MESH,
        )

    for step in range(1, n_inner):
        line_copy(step, me_i).start()

    for copy in loads[H_MID + 1]:
        copy.wait()

    def near_head(head):
        columns = slice(head * HEAD_DIM, (head + 1) * HEAD_DIM)
        q, k, v, g = [x[a, :, columns] for a in range(4)]
        weights, score_grads = attention_parts(q, k, v, g)
        outputs[0][:, columns] = dot(score_grads, k, (0, 0)).astype(BF16)
        outputs[1][:, columns] = dot(score_grads, q, (1, 0)).astype(BF16)
        outputs[2][:, columns] = dot(weights, g, (1, 0)).astype(BF16)

    def back_copy(slot, head, source, which):
        return pltpu.make_async_remote_copy(
            src_ref=result.at[slot, source, which], dst_ref=returned.at[head, which],
            send_sem=back_send.at[slot, source, which], recv_sem=back_recv.at[head, which],
            device_id=(me_o, source), device_id_type=MESH,
        )

    def owned(slot):
        if slot == 0:
            return me_i
        shift = lax.rem(me_i + 2 * n_inner - n_inner // 2 + lax.rem(me_o, 2), n_inner)
        return slot * n_inner + shift

    def back_peer(step):
        return inner_peer(jnp.where(lax.rem(me_i, 2) == 0, step, n_inner - step))

    segment = n_inner * rows

    def own_slot(slot):
        head = owned(slot)

        @pl.when(head < H_MID)
        def _():
            for step in range(1, n_inner):
                source = inner_peer(step)
                mid_copy(0, slot, source, source).wait_recv()
            q, k, v, g = [arrived[slot, :, a].reshape(segment, HEAD_DIM) for a in range(4)]
            weights, score_grads = attention_parts(q, k, v, g)
            for which, left, right, contract in (
                (2, weights, g, (1, 0)), (1, score_grads, q, (1, 0)), (0, score_grads, k, (0, 0))
            ):
                grads = dot(left, right, contract).astype(BF16)
                result[slot, :, which] = grads.reshape(n_inner, rows, HEAD_DIM)
                for step in (*range(n_inner // 2, n_inner), *range(1, n_inner // 2)):
                    back_copy(slot, head, back_peer(step), which).start()
                returned[head, which] = result[slot, me_i, which]

    def first_near():
        for head in range(H_NEAR // 2):
            near_head(head)

    several = owned(slots - 1) < H_MID if slots > 1 else me_i < 0
    pl.when(jnp.logical_not(several))(first_near)
    for slot in reversed(range(1, slots)):
        own_slot(slot)

    own_slot(0)

    for step in range(1, n_inner):
        line_copy(step, inner_peer(step)).wait_recv()

    def plane_copy(step, source):
        return pltpu.make_async_remote_copy(
            src_ref=wide.at[me_o], dst_ref=wide.at[source],
            send_sem=plane_send.at[step], recv_sem=plane_recv.at[source],
            device_id=(outer_peer(step), me_i), device_id_type=MESH,
        )

    for step in range(1, n_outer):
        plane_copy(step, me_o).start()

    pl.when(several)(first_near)
    for head in range(H_NEAR // 2, H_NEAR):
        near_head(head)

    for step in range(1, n_outer):
        plane_copy(step, outer_peer(step)).wait_recv()
    devices = n_outer * n_inner
    total = devices * WIDE_ROWS
    tile = min(total, 256)

    def gathered(a, start, count):
        block = wide[...].reshape(devices, 4 * WIDE_ROWS, HEAD_DIM).astype(F32)
        return block[start:start + count, a * WIDE_ROWS:(a + 1) * WIDE_ROWS].reshape(
            count * WIDE_ROWS, HEAD_DIM).astype(BF16)

    wide_k, wide_v = gathered(1, 0, devices), gathered(2, 0, devices)
    wide_result[...] = jnp.zeros_like(wide_result)
    for first in range(0, total, tile):
        q = gathered(0, first // WIDE_ROWS, tile // WIDE_ROWS)
        g = gathered(3, first // WIDE_ROWS, tile // WIDE_ROWS)
        key_head = lax.rem(lax.broadcasted_iota(jnp.int32, (total, 1), 0), WIDE_ROWS) // wide_tokens
        query_head = lax.rem(lax.broadcasted_iota(jnp.int32, (1, tile), 1), WIDE_ROWS) // wide_tokens
        weights, score_grads = attention_parts(q, wide_k, wide_v, g, key_head == query_head)
        wide_result[0, first:first + tile] = dot(score_grads, wide_k, (0, 0))
        wide_result[1] += dot(score_grads, q, (1, 0))
        wide_result[2] += dot(weights, g, (1, 0))
    mine = pl.ds(pl.multiple_of((me_o * n_inner + me_i) * WIDE_ROWS, WIDE_ROWS), WIDE_ROWS)
    place = lax.broadcasted_iota(jnp.int32, (tokens, HEAD_DIM), 0)
    for which in range(3):
        block = wide_result[which, mine, :]
        for head in range(H_WIDE):
            spread = jnp.zeros((tokens, HEAD_DIM), F32)
            for token in range(wide_tokens):
                at = head * wide_tokens + token
                spread = jnp.where(
                    place == token * R_WIDE + offsets[H_MID + head], block[at:at + 1], spread
                )
            first = MID_END + head * HEAD_DIM
            outputs[which][:, first:first + HEAD_DIM] = spread.astype(BF16)

    spread_row = lax.broadcasted_iota(jnp.int32, (tokens, rows), 1)
    spread_position = lax.broadcasted_iota(jnp.int32, (tokens, rows), 0)
    returning = [lax.rem(me_i + step, H_MID - 1) for step in (0, 1, 3, 2)]
    for head in (returning[0], jnp.int32(H_MID - 1), *returning[1:]):
        target = owner(head)
        place = (spread_position == spread_row * R_MID + offsets[head]).astype(F32).astype(BF16)
        columns = head_columns(head)
        for which in (2, 1, 0):

            @pl.when(me_i != target)
            def _():
                back_copy(0, head, target, which).wait_recv()

            outputs[which][:, columns] = dot(place, returned[head, which], (1, 0)).astype(BF16)

    for step in range(1, n_inner):
        line_copy(step, me_i).wait_send()
    for step in range(1, n_outer):
        plane_copy(step, me_o).wait_send()
    for head in range(H_MID):
        target = owner(head)

        @pl.when(me_i != target)
        def _():
            mid_copy(head, 0, me_i, target).wait_send()

    for slot in range(slots):
        head = owned(slot)

        @pl.when(head < H_MID)
        def _():
            for step in range(1, n_inner):
                for which in range(3):
                    back_copy(slot, head, inner_peer(step), which).wait_send()


def write_out(grads):
    pieces = 4

    def copies(*refs):
        sems = refs[6]
        step = refs[0].shape[0] // pieces
        started = []
        for which in range(3):
            for piece in range(pieces):
                part = pl.ds(piece * step, step)
                copy = pltpu.make_async_copy(
                    refs[which].at[part], refs[3 + which].at[part], sems.at[which, piece]
                )
                copy.start()
                started.append(copy)
        for copy in started:
            copy.wait()

    return tuple(pl.pallas_call(
        copies,
        out_shape=[jax.ShapeDtypeStruct(grad.shape, grad.dtype) for grad in grads],
        in_specs=[pl.BlockSpec(memory_space=pltpu.VMEM)] * 3,
        out_specs=[pl.BlockSpec(memory_space=pltpu.HBM)] * 3,
        scratch_shapes=[pltpu.SemaphoreType.DMA((3, pieces))],
        compiler_params=pltpu.CompilerParams(vmem_limit_bytes=16 * 1024 * 1024),
    )(*[pltpu.with_memory_space_constraint(grad, pltpu.VMEM) for grad in grads]))


def body(n_outer, n_inner, queries, key_rows, values, out_grads, offsets):
    tokens, columns = queries.shape
    rows = tokens // R_MID
    slots = -(-H_MID // n_inner)
    dma = pltpu.SemaphoreType.DMA
    grads = pl.pallas_call(
        functools.partial(kernel, n_outer, n_inner),
        out_shape=[jax.ShapeDtypeStruct((tokens, columns), BF16)] * 3,
        in_specs=[pl.BlockSpec(memory_space=pltpu.HBM)] * 5,
        out_specs=[pl.BlockSpec(memory_space=pltpu.VMEM)] * 3,
        scratch_shapes=[
            pltpu.SMEM(offsets.shape, jnp.int32),
            pltpu.VMEM((4, tokens, columns), BF16),
            pltpu.VMEM((H_MID, 4, rows, HEAD_DIM), BF16),
            pltpu.VMEM((slots, n_inner, 4, rows, HEAD_DIM), BF16),
            pltpu.VMEM((slots, n_inner, 3, rows, HEAD_DIM), BF16),
            pltpu.VMEM((H_MID, 3, rows, HEAD_DIM), BF16),
            pltpu.VMEM((n_outer, n_inner, 4 * WIDE_ROWS, HEAD_DIM), BF16),
            pltpu.VMEM((3, n_outer * n_inner * WIDE_ROWS, HEAD_DIM), F32),
            dma,
            dma((H_MID + 2, 4)),
            dma((H_MID,)),
            dma((slots, n_inner)),
            dma((slots, n_inner, 3)),
            dma((H_MID, 3)),
            dma((n_inner,)),
            dma((n_inner,)),
            dma((n_outer,)),
            dma((n_outer,)),
        ],
        compiler_params=pltpu.CompilerParams(
            collective_id=0, has_side_effects=True, vmem_limit_bytes=48 * 1024 * 1024
        ),
    )(*[pltpu.with_memory_space_constraint(a, pltpu.HBM) for a in (offsets, queries, key_rows, values, out_grads)])
    return write_out(grads)


def solution(mesh):
    split = P(("outer", "inner"), None)
    return jax.shard_map(
        functools.partial(body, mesh.shape["outer"], mesh.shape["inner"]),
        mesh=mesh,
        in_specs=(split, split, split, split, P()),
        out_specs=(split,) * 3,
        check_vma=False,
    )
```

```python
import functools
import math

import jax
import jax.numpy as jnp
from jax import lax
from jax.experimental import pallas as pl
from jax.experimental.pallas import tpu as pltpu
from jax.sharding import PartitionSpec as P

HEAD_DIM = 128
H_NEAR = 4
H_MID = 5
H_WIDE = 3
HEADS = H_NEAR + H_MID + H_WIDE
R_MID = 4
R_WIDE = 128
NEAR_END = H_NEAR * HEAD_DIM
MID_END = NEAR_END + H_MID * HEAD_DIM
WIDE_ROWS = 8
MESH = pl.DeviceIdType.MESH
F32 = jnp.float32
BF16 = jnp.bfloat16


def dot(left, right, contract):
    return lax.dot_general(left, right, ((contract[:1], contract[1:]), ((), ())), preferred_element_type=F32)


def attention_parts(q, k, v, g, mask=None):
    scale = 1.0 / math.sqrt(HEAD_DIM)
    scores = dot(k, q, (1, 1)) * scale
    if mask is not None:
        scores = jnp.where(mask, scores, -1e30)
    exponent = jnp.exp(scores - jnp.max(scores, axis=0, keepdims=True))
    weights = exponent * (1.0 / jnp.sum(exponent, axis=0, keepdims=True))
    dots = dot(v, g, (1, 1))
    row_dots = jnp.sum(weights * dots, axis=0, keepdims=True)
    score_grads = (weights * (dots - row_dots) * scale).astype(BF16)
    return weights.astype(BF16), score_grads


def kernel(
    n_outer, n_inner, offsets_in, queries, key_rows, values, out_grads, grad_q, grad_k, grad_v,
    offsets, x, picked, arrived, result, returned, wide, wide_result,
    offsets_sem, in_sem, mid_send, mid_recv, back_send, back_recv,
    line_send, line_recv, plane_send, plane_recv,
):
    tokens = x.shape[1]
    rows = tokens // R_MID
    wide_tokens = tokens // R_WIDE
    slots = arrived.shape[0]
    me_o, me_i = lax.axis_index("outer"), lax.axis_index("inner")
    inputs = (queries, key_rows, values, out_grads)
    outputs = (grad_q, grad_k, grad_v)

    def inner_peer(step):
        return lax.rem(me_i + step, n_inner)

    def outer_peer(step):
        return lax.rem(me_o + step, n_outer)

    barrier = pltpu.get_barrier_semaphore()
    for step in range(1, n_inner):
        pl.semaphore_signal(barrier, inc=1, device_id=(me_o, inner_peer(step)), device_id_type=MESH)
    for step in range(1, n_outer):
        pl.semaphore_signal(barrier, inc=1, device_id=(outer_peer(step), me_i), device_id_type=MESH)

    left = me_i < n_inner // 2
    half = (H_MID - 1) // 2

    def head_at(step):
        if step == 0:
            return jnp.int32(H_MID - 1)
        return jnp.where(
            left, lax.rem(half + step - 1, H_MID - 1), lax.rem(half + H_MID - 1 - step, H_MID - 1)
        )

    def head_columns(head):
        return pl.ds(pl.multiple_of(NEAR_END + head * HEAD_DIM, HEAD_DIM), HEAD_DIM)

    def load(group, span):
        return [
            pltpu.make_async_copy(inputs[a].at[:, span], x.at[a, :, span], in_sem.at[group, a])
            for a in range(4)
        ]

    near_span, wide_span = pl.ds(0, NEAR_END), pl.ds(MID_END, H_WIDE * HEAD_DIM)
    offsets_load = pltpu.make_async_copy(offsets_in, offsets, offsets_sem)
    offsets_load.start()
    loads = [load(step, head_columns(head_at(step))) for step in range(H_MID)]
    loads += [load(H_MID, wide_span), load(H_MID + 1, near_span)]
    for group in (0, 1, H_MID, *range(2, H_MID), H_MID + 1):
        for copy in loads[group]:
            copy.start()

    def owner(head):
        turned = head + n_inner // 2 + n_inner - lax.rem(me_o, 2)
        return jnp.where(head < n_inner, head, lax.rem(turned, n_inner))

    def mid_copy(head, slot, source, target):
        return pltpu.make_async_remote_copy(
            src_ref=picked.at[head], dst_ref=arrived.at[slot, source],
            send_sem=mid_send.at[head], recv_sem=mid_recv.at[slot, source],
            device_id=(me_o, target), device_id_type=MESH,
        )

    pick_row = lax.broadcasted_iota(jnp.int32, (rows, tokens), 0)
    pick_position = lax.broadcasted_iota(jnp.int32, (rows, tokens), 1)

    def pick_head(step):
        for copy in loads[step]:
            copy.wait()
        head = head_at(step)
        pick = (pick_position == pick_row * R_MID + offsets[head]).astype(F32).astype(BF16)
        for a in range(4):
            picked[head, a] = dot(pick, x[a, :, head_columns(head)], (1, 0)).astype(BF16)

    def send_head(step):
        head = head_at(step)
        target, slot = owner(head), head // n_inner

        @pl.when(me_i != target)
        def _():
            mid_copy(head, slot, me_i, target).start()

        @pl.when(me_i == target)
        def _():
            arrived[slot, me_i] = picked[head]

    offsets_load.wait()
    pick_head(0)
    pl.semaphore_wait(barrier, n_inner - 1 + n_outer - 1)
    send_head(0)
    pick_head(1)
    send_head(1)

    for copy in loads[H_MID]:
        copy.wait()
    position = lax.broadcasted_iota(jnp.int32, (16, tokens), 1)
    row = lax.broadcasted_iota(jnp.int32, (16, tokens), 0)
    chosen = jnp.zeros((16, tokens), jnp.bool_)
    for head in range(H_WIDE):
        for token in range(wide_tokens):
            at = token * R_WIDE + offsets[H_MID + head]
            chosen = chosen | ((row == head * wide_tokens + token) & (position == at))
    chosen = chosen.astype(F32).astype(BF16)
    head_of = lax.broadcasted_iota(jnp.int32, (WIDE_ROWS, HEAD_DIM), 0) // wide_tokens
    blocks = []
    for a in range(4):
        both = dot(chosen, x[a, :, MID_END:], (1, 0))[:WIDE_ROWS]
        block = jnp.zeros((WIDE_ROWS, HEAD_DIM), F32)
        for head in range(H_WIDE):
            part = both[:, head * HEAD_DIM:(head + 1) * HEAD_DIM]
            block = jnp.where(head_of == head, part, block)
        blocks.append(block)
    wide[me_o, me_i] = jnp.concatenate(blocks, axis=0).astype(BF16)

    def line_copy(step, source):
        return pltpu.make_async_remote_copy(
            src_ref=wide.at[me_o, me_i], dst_ref=wide.at[me_o, source],
            send_sem=line_send.at[step], recv_sem=line_recv.at[source],
            device_id=(me_o, inner_peer(step)), device_id_type=MESH,
        )

    for step in range(1, n_inner):
        line_copy(step, me_i).start()

    for step in range(2, H_MID):
        pick_head(step)
        send_head(step)

    for copy in loads[H_MID + 1]:
        copy.wait()

    def near_head(head):
        columns = slice(head * HEAD_DIM, (head + 1) * HEAD_DIM)
        q, k, v, g = [x[a, :, columns] for a in range(4)]
        weights, score_grads = attention_parts(q, k, v, g)
        outputs[0][:, columns] = dot(score_grads, k, (0, 0)).astype(BF16)
        outputs[1][:, columns] = dot(score_grads, q, (1, 0)).astype(BF16)
        outputs[2][:, columns] = dot(weights, g, (1, 0)).astype(BF16)

    def back_copy(slot, head, source):
        return pltpu.make_async_remote_copy(
            src_ref=result.at[slot, source], dst_ref=returned.at[head],
            send_sem=back_send.at[slot, source], recv_sem=back_recv.at[head],
            device_id=(me_o, source), device_id_type=MESH,
        )

    def owned(slot):
        if slot == 0:
            return me_i
        shift = lax.rem(me_i + 2 * n_inner - n_inner // 2 + lax.rem(me_o, 2), n_inner)
        return slot * n_inner + shift

    def back_peer(step):
        return inner_peer(jnp.where(lax.rem(me_i, 2) == 0, step, n_inner - step))

    segment = n_inner * rows

    def own_slot(slot):
        head = owned(slot)

        @pl.when(head < H_MID)
        def _():
            for step in range(1, n_inner):
                source = inner_peer(step)
                mid_copy(0, slot, source, source).wait_recv()
            q, k, v, g = [arrived[slot, :, a].reshape(segment, HEAD_DIM) for a in range(4)]
            weights, score_grads = attention_parts(q, k, v, g)
            for which, left, right, contract in (
                (2, weights, g, (1, 0)), (1, score_grads, q, (1, 0)), (0, score_grads, k, (0, 0))
            ):
                grads = dot(left, right, contract).astype(BF16)
                result[slot, :, which] = grads.reshape(n_inner, rows, HEAD_DIM)
            for step in (*range(n_inner // 2, n_inner), *range(1, n_inner // 2)):
                back_copy(slot, head, back_peer(step)).start()
            returned[head] = result[slot, me_i]

    def near_heads(*heads):
        for head in heads:
            near_head(head)

    first_near = functools.partial(near_heads, *range(H_NEAR // 2))
    second_near = functools.partial(near_heads, *range(H_NEAR // 2, H_NEAR))

    several = owned(slots - 1) < H_MID if slots > 1 else me_i < 0
    pl.when(jnp.logical_not(several))(first_near)
    for slot in reversed(range(1, slots)):
        own_slot(slot)

    for step in range(1, n_inner):
        line_copy(step, inner_peer(step)).wait_recv()

    def plane_copy(step, source):
        return pltpu.make_async_remote_copy(
            src_ref=wide.at[me_o], dst_ref=wide.at[source],
            send_sem=plane_send.at[step], recv_sem=plane_recv.at[source],
            device_id=(outer_peer(step), me_i), device_id_type=MESH,
        )

    for step in range(1, n_outer):
        plane_copy(step, me_o).start()

    pl.when(jnp.logical_not(several))(second_near)
    own_slot(0)
    pl.when(several)(functools.partial(near_heads, *range(H_NEAR)))

    for step in range(1, n_outer):
        plane_copy(step, outer_peer(step)).wait_recv()
    devices = n_outer * n_inner
    total = devices * WIDE_ROWS
    tile = min(total, 256)

    def gathered(a, start, count):
        block = wide[...].reshape(devices, 4 * WIDE_ROWS, HEAD_DIM).astype(F32)
        return block[start:start + count, a * WIDE_ROWS:(a + 1) * WIDE_ROWS].reshape(
            count * WIDE_ROWS, HEAD_DIM).astype(BF16)

    wide_k, wide_v = gathered(1, 0, devices), gathered(2, 0, devices)
    wide_result[...] = jnp.zeros_like(wide_result)
    for first in range(0, total, tile):
        q = gathered(0, first // WIDE_ROWS, tile // WIDE_ROWS)
        g = gathered(3, first // WIDE_ROWS, tile // WIDE_ROWS)
        key_head = lax.rem(lax.broadcasted_iota(jnp.int32, (total, 1), 0), WIDE_ROWS) // wide_tokens
        query_head = lax.rem(lax.broadcasted_iota(jnp.int32, (1, tile), 1), WIDE_ROWS) // wide_tokens
        weights, score_grads = attention_parts(q, wide_k, wide_v, g, key_head == query_head)
        wide_result[0, first:first + tile] = dot(score_grads, wide_k, (0, 0))
        wide_result[1] += dot(score_grads, q, (1, 0))
        wide_result[2] += dot(weights, g, (1, 0))
    mine = pl.ds(pl.multiple_of((me_o * n_inner + me_i) * WIDE_ROWS, WIDE_ROWS), WIDE_ROWS)
    place = lax.broadcasted_iota(jnp.int32, (tokens, HEAD_DIM), 0)
    for which in range(3):
        block = wide_result[which, mine, :]
        for head in range(H_WIDE):
            spread = jnp.zeros((tokens, HEAD_DIM), F32)
            for token in range(wide_tokens):
                at = head * wide_tokens + token
                spread = jnp.where(
                    place == token * R_WIDE + offsets[H_MID + head], block[at:at + 1], spread
                )
            first = MID_END + head * HEAD_DIM
            outputs[which][:, first:first + HEAD_DIM] = spread.astype(BF16)

    spread_row = lax.broadcasted_iota(jnp.int32, (tokens, rows), 1)
    spread_position = lax.broadcasted_iota(jnp.int32, (tokens, rows), 0)
    returning = [lax.rem(me_i + step, H_MID - 1) for step in (0, 1, 3, 2)]
    for group in ((returning[0], jnp.int32(H_MID - 1), returning[1]), returning[2:]):
        for head in group:
            target = owner(head)

            @pl.when(me_i != target)
            def _():
                back_copy(0, head, target).wait_recv()

        for head in group:
            place = (spread_position == spread_row * R_MID + offsets[head]).astype(F32).astype(BF16)
            for which in range(3):
                outputs[which][:, head_columns(head)] = dot(
                    place, returned[head, which], (1, 0)
                ).astype(BF16)

    for step in range(1, n_inner):
        line_copy(step, me_i).wait_send()
    for step in range(1, n_outer):
        plane_copy(step, me_o).wait_send()
    for head in range(H_MID):
        target = owner(head)

        @pl.when(me_i != target)
        def _():
            mid_copy(head, 0, me_i, target).wait_send()

    for slot in range(slots):
        head = owned(slot)

        @pl.when(head < H_MID)
        def _():
            for step in range(1, n_inner):
                back_copy(slot, head, inner_peer(step)).wait_send()


def write_out(grads):
    pieces = 4

    def copies(*refs):
        sems = refs[6]
        step = refs[0].shape[0] // pieces
        started = []
        for which in range(3):
            for piece in range(pieces):
                part = pl.ds(piece * step, step)
                copy = pltpu.make_async_copy(
                    refs[which].at[part], refs[3 + which].at[part], sems.at[which, piece]
                )
                copy.start()
                started.append(copy)
        for copy in started:
            copy.wait()

    return tuple(pl.pallas_call(
        copies,
        out_shape=[jax.ShapeDtypeStruct(grad.shape, grad.dtype) for grad in grads],
        in_specs=[pl.BlockSpec(memory_space=pltpu.VMEM)] * 3,
        out_specs=[pl.BlockSpec(memory_space=pltpu.HBM)] * 3,
        scratch_shapes=[pltpu.SemaphoreType.DMA((3, pieces))],
        compiler_params=pltpu.CompilerParams(vmem_limit_bytes=16 * 1024 * 1024),
    )(*[pltpu.with_memory_space_constraint(grad, pltpu.VMEM) for grad in grads]))


def body(n_outer, n_inner, queries, key_rows, values, out_grads, offsets):
    tokens, columns = queries.shape
    rows = tokens // R_MID
    slots = -(-H_MID // n_inner)
    dma = pltpu.SemaphoreType.DMA
    grads = pl.pallas_call(
        functools.partial(kernel, n_outer, n_inner),
        out_shape=[jax.ShapeDtypeStruct((tokens, columns), BF16)] * 3,
        in_specs=[pl.BlockSpec(memory_space=pltpu.HBM)] * 5,
        out_specs=[pl.BlockSpec(memory_space=pltpu.VMEM)] * 3,
        scratch_shapes=[
            pltpu.SMEM(offsets.shape, jnp.int32),
            pltpu.VMEM((4, tokens, columns), BF16),
            pltpu.VMEM((H_MID, 4, rows, HEAD_DIM), BF16),
            pltpu.VMEM((slots, n_inner, 4, rows, HEAD_DIM), BF16),
            pltpu.VMEM((slots, n_inner, 3, rows, HEAD_DIM), BF16),
            pltpu.VMEM((H_MID, 3, rows, HEAD_DIM), BF16),
            pltpu.VMEM((n_outer, n_inner, 4 * WIDE_ROWS, HEAD_DIM), BF16),
            pltpu.VMEM((3, n_outer * n_inner * WIDE_ROWS, HEAD_DIM), F32),
            dma,
            dma((H_MID + 2, 4)),
            dma((H_MID,)),
            dma((slots, n_inner)),
            dma((slots, n_inner)),
            dma((H_MID,)),
            dma((n_inner,)),
            dma((n_inner,)),
            dma((n_outer,)),
            dma((n_outer,)),
        ],
        compiler_params=pltpu.CompilerParams(
            collective_id=0, has_side_effects=True, vmem_limit_bytes=48 * 1024 * 1024
        ),
    )(*[pltpu.with_memory_space_constraint(a, pltpu.HBM) for a in (offsets, queries, key_rows, values, out_grads)])
    return write_out(grads)


def solution(mesh):
    split = P(("outer", "inner"), None)
    return jax.shard_map(
        functools.partial(body, mesh.shape["outer"], mesh.shape["inner"]),
        mesh=mesh,
        in_specs=(split, split, split, split, P()),
        out_specs=(split,) * 3,
        check_vma=False,
    )
```
